32 devices in a mesh: feat: 4 (over y, x), rows: 8 (over z, core).
Axes of the slice: x: 2, y: 2, z: 4, core: 2. Of those that a mesh axis runs over, the one named last changes fastest.
Arguments:
- features: bfloat16 [2, 32768, 100], P(None, 'rows', 'feat'), may hold values from -6 to 6
- feat_mask: int32 [2, 32768, 100], P(None, 'rows', 'feat'), may hold values 0 or 1
- send_order: int32 [2, 8, 4, 1024], P(None, 'rows', 'feat'), may hold values from 0 to 1023, each once within a row
- segment: int32 [2, 4, 8, 1024], P(None, 'feat', 'rows'), may hold values from 0 to 1, as said below
- context: int32 [2, 4, 8, 1024], P(None, 'feat', 'rows'), may hold values 0 or 1
- cotangent: bfloat16 [2, 4, 8192, 512], P(None, 'feat', 'rows'), may hold values from -6 to 6
- w_enc: float32 [100, 512], P(None, 'rows'), may hold values from -0.625 to 0.625
- w_attn: float32 [512, 2048], P('rows')
- w_ffn: float32 [512, 2048], P('rows')
- vectors: float32 [6, 512], P(None, 'rows'), as said below
- m_enc: float32 [100, 512], P(None, 'rows'), as said below
- v_enc: float32 [100, 512], P(None, 'rows'), may hold values from 3449 to 13797
- m_attn: float32 [512, 2048], P('rows'), as said below
- v_attn: float32 [512, 2048], P('rows'), may hold values from 862 to 3449
- m_ffn: float32 [512, 2048], P('rows'), as said below
- v_ffn: float32 [512, 2048], P('rows'), may hold values from 1724 to 6898
- m_vec: float32 [6, 512], P(None, 'rows')
- v_vec: float32 [6, 512], P(None, 'rows'), may hold values from 3449 to 13797
Outputs:
- activations: float32 [2, 4, 8192, 512], P(None, 'feat', 'rows')
- x_grad: float32 [2, 32768, 100], P(None, 'rows', 'feat')
- w_enc_new: float32 [100, 512], P(None, 'rows')
- m_enc_new: float32 [100, 512], P(None, 'rows')
- v_enc_new: float32 [100, 512], P(None, 'rows')
- w_attn_new: float32 [512, 2048], P('rows')
- m_attn_new: float32 [512, 2048], P('rows')
- v_attn_new: float32 [512, 2048], P('rows')
- w_ffn_new: float32 [512, 2048], P('rows')
- m_ffn_new: float32 [512, 2048], P('rows')
- v_ffn_new: float32 [512, 2048], P('rows')
- vectors_new: float32 [6, 512], P(None, 'rows')
- m_vec_new: float32 [6, 512], P(None, 'rows')
- v_vec_new: float32 [6, 512], P(None, 'rows')
The draws below stay inside these ranges and needn't reach their ends.
Inputs may be any that keep to these rules, and one draw needn't show every extreme that they name: `segment`: each device's group holds two neighbourhoods in order of position, one of 768 and one of 256 positions, the larger first or second. `m_enc`: first moments are of either sign. `m_attn`: first moments are of either sign. `m_ffn`: first moments are of either sign. `vectors`: row 1 and row 3 are gains near 1.
All inputs are finite; a program needn't handle non-finite values. No bound on the sum of `feat_mask` or of `context` on one device may be relied on, other than what follows from the above.
Results may differ from the reference program's by a relative error of at most 0.015.
Values may be sent and summed in bfloat16 or wider, within the bound.
No kernel may reach another device: no remote copies, remote signals or barrier semaphores. Data moves between devices by JAX's collectives and lax.ppermute only.
A program may use at most 192 MiB of HBM per device.

```python
import math
import jax
import jax.numpy as jnp
from jax import lax

D = 512
HEADS = 4
FF = 1024
F = 100
TD = 1024
M = 2
STEP = 10
HD = 128
ROWS_ALL = 32768
POST = 8192
TOKENS_ALL = 65536
N_FEAT = 4
N_ROWS = 8


def bounded_normal(key, shape):
    return jax.random.truncated_normal(key, -4.0, 4.0, shape, jnp.float32)


def draw_segment(key, part):
    large_first = jax.random.randint(jax.random.fold_in(key, 31), (M, N_FEAT, N_ROWS, 1), 0, 2)
    boundary = jnp.where(large_first == 1, 3 * TD // 4, TD // 4)
    places = jnp.arange(TD)[None, None, None, :]
    return (places >= boundary).astype(jnp.int32)


def draw_w_attn(key, part):
    inner_key, outer_key = jax.random.split(jax.random.fold_in(key, 11))
    inner = bounded_normal(inner_key, (D, 3 * D)) * D ** (-0.5)
    outer = bounded_normal(outer_key, (D, D)) * math.sqrt(TD / (4.0 * D))
    return jnp.concatenate([inner, outer], axis=1)


def draw_w_ffn(key, part):
    up_key, down_key = jax.random.split(jax.random.fold_in(key, 12))
    up_part = bounded_normal(up_key, (D, FF)) * D ** (-0.5)
    down_part = bounded_normal(down_key, (D, FF)) * FF ** (-0.5)
    return jnp.concatenate([up_part, down_part], axis=1)


def draw_vectors(key, part):
    normal_key, gain_key = jax.random.split(jax.random.fold_in(key, 13))
    shifts = bounded_normal(normal_key, (6, D)) * jnp.array([0.5, 0.0, 0.3, 0.0, 0.3, 0.3], jnp.float32)[:, None]
    gains = 1.0 + jax.random.uniform(gain_key, (6, D), jnp.float32, -0.3, 0.3)
    is_gain = jnp.array([0.0, 1.0, 0.0, 1.0, 0.0, 0.0], jnp.float32)[:, None]
    return shifts * (1.0 - is_gain) + gains * is_gain


def draw_m_enc(key, part):
    return bounded_normal(jax.random.fold_in(key, 21), (F, D)) * (math.sqrt(TOKENS_ALL) / 9.0)


def draw_m_attn(key, part):
    return bounded_normal(jax.random.fold_in(key, 22), (D, 4 * D)) * (0.5 * math.sqrt(TOKENS_ALL) / 9.0)


def draw_m_ffn(key, part):
    return bounded_normal(jax.random.fold_in(key, 23), (D, 2 * FF)) * (0.7 * math.sqrt(TOKENS_ALL) / 9.0)


def draw_m_vec(key, part):
    return bounded_normal(jax.random.fold_in(key, 24), (6, D)) * (math.sqrt(TOKENS_ALL) / 9.0)


def set_ends(entries, rng, least, high):
    place = [jax.random.randint(jax.random.fold_in(rng, axis), (), 0, length) for axis, length in enumerate(entries.shape)]
    longest = entries.shape.index(max(entries.shape))
    neighbour = place[:longest] + [(place[longest] + 1) % entries.shape[longest]] + place[longest + 1:]
    return entries.at[tuple(place)].set(least).at[tuple(neighbour)].set(high)


def shard_levels(key, extent, pieces, smallest, top_value):
    def one(position, shards_of):
        steps = jax.random.uniform(jax.random.fold_in(jax.random.fold_in(key, 6), position), (shards_of,), jnp.float32, smallest / len(pieces), top_value / len(pieces))
        return jnp.repeat(jnp.exp(steps), extent[position] // shards_of).reshape((-1,) + (1,) * (len(extent) - position - 1))

    loudness = one(*pieces[0])
    for cut in pieces[1:]:
        loudness = loudness * one(*cut)
    return loudness


def normal_values(key, shape, scale, most, cuts=(), kind=jnp.bfloat16):
    drawn = scale * jax.random.normal(key, shape, jnp.float32)
    if cuts:
        drawn = drawn * shard_levels(key, shape, cuts, -0.22, 0.18)
    return jnp.clip(drawn, -most, most).astype(kind)


def setup_inputs(seed: int = 0) -> dict:
    keys = jax.random.split(jax.random.key(seed), 19)
    features = normal_values(keys[0], (M, ROWS_ALL, F), 1.0, 6.0, ((1, 8), (2, 4)))
    feat_mask = set_ends((jax.random.randint(keys[1], (M, ROWS_ALL, F), 0, 5) < 4).astype(jnp.int32), jax.random.fold_in(keys[1], 1), 0, 1)
    send_order = jax.vmap(lambda own: jax.random.permutation(own, TD))(jax.random.split(keys[2], M * N_ROWS * N_FEAT)).reshape((M, N_ROWS, N_FEAT, TD)).astype(jnp.int32)
    segment = draw_segment(jax.random.fold_in(keys[18], 71), 0)
    context = set_ends((jax.random.randint(keys[4], (M, N_FEAT, N_ROWS, TD), 0, 4) < 3).astype(jnp.int32), jax.random.fold_in(keys[4], 1), 0, 1)
    cotangent = normal_values(keys[5], (M, N_FEAT, POST, D), 1.0, 6.0, ((1, 4), (2, 8)))
    w_enc = normal_values(keys[6], (F, D), F ** -0.5, 0.625, ((1, 8),), jnp.float32)
    w_attn = draw_w_attn(jax.random.fold_in(keys[18], 71), 0)
    w_ffn = draw_w_ffn(jax.random.fold_in(keys[18], 71), 0)
    vectors = draw_vectors(jax.random.fold_in(keys[18], 71), 0)
    m_enc = draw_m_enc(jax.random.fold_in(keys[18], 71), 0)
    v_enc = jnp.clip(jnp.exp(math.log(13797.0) - 1.3863668 * jax.random.uniform(keys[11], (F, D), jnp.float32) ** shard_levels(keys[11], (F, D), ((1, 8),), -0.2, 0.2)), 3449.0, 13797.0)
    m_attn = draw_m_attn(jax.random.fold_in(keys[18], 71), 0)
    v_attn = jnp.clip(jnp.exp(math.log(3449.0) - 1.3865843422731479 * jax.random.uniform(keys[13], (D, 4 * D), jnp.float32) ** shard_levels(keys[13], (D, 4 * D), ((0, 8),), -0.2, 0.2)), 862.0, 3449.0)
    m_ffn = draw_m_ffn(jax.random.fold_in(keys[18], 71), 0)
    v_ffn = jnp.clip(jnp.exp(math.log(6898.0) - 1.3865843422731479 * jax.random.uniform(keys[15], (D, 2 * FF), jnp.float32) ** shard_levels(keys[15], (D, 2 * FF), ((0, 8),), -0.2, 0.2)), 1724.0, 6898.0)
    m_vec = draw_m_vec(jax.random.fold_in(keys[18], 71), 0)
    v_vec = jnp.clip(jnp.exp(math.log(13797.0) - 1.3863668 * jax.random.uniform(keys[17], (6, D), jnp.float32) ** shard_levels(keys[17], (6, D), ((1, 8),), -0.2, 0.2)), 3449.0, 13797.0)
    return dict(features=features, feat_mask=feat_mask, send_order=send_order, segment=segment, context=context, cotangent=cotangent, w_enc=w_enc, w_attn=w_attn, w_ffn=w_ffn, vectors=vectors, m_enc=m_enc, v_enc=v_enc, m_attn=m_attn, v_attn=v_attn, m_ffn=m_ffn, v_ffn=v_ffn, m_vec=m_vec, v_vec=v_vec)


@jax.custom_vjp
def low(v):
    return lax.optimization_barrier(v.astype(jnp.bfloat16)).astype(jnp.float32)

@jax.custom_vjp
def low_back(v):
    return v

def low_keep(v):
    return (low(v), None)

def low_pass(kept, grad):
    return (grad,)

def back_keep(v):
    return (v, None)

def back_low(kept, grad):
    return (low(grad),)
low.defvjp(low_keep, low_pass)
low_back.defvjp(back_keep, back_low)
highest = lax.Precision.HIGHEST
encoder_rate = 0.08
attention_rate = 0.25
feedforward_rate = 0.02
vector_rate = 0.2

def layer_norm(inputs, gain, shift):
    average = lax.optimization_barrier(jnp.mean(inputs, axis=-1, keepdims=True))
    centred = inputs - average
    variance = lax.optimization_barrier(jnp.mean(centred * centred, axis=-1, keepdims=True))
    return centred * lax.rsqrt(variance + 1e-05) * gain + shift

def adamw(weight, gradient, first, second, rate):
    first_new = 0.9 * first + 0.1 * gradient
    second_new = 0.95 * second + 0.05 * gradient * gradient
    corrected = first_new / (1.0 - 0.9 ** STEP) / (jnp.sqrt(second_new / (1.0 - 0.95 ** STEP)) + 1e-08)
    return (weight - rate * (corrected + 0.1 * weight), first_new, second_new)

def attend(group_rows, seg_rows, ctx_rows, qkv_weight):
    length = group_rows.shape[0]
    qkv = low_back(low(jnp.dot(group_rows, qkv_weight, precision=highest)))
    queries = qkv[:, :D].reshape(length, HEADS, HD)
    key_rows = qkv[:, D:2 * D].reshape(length, HEADS, HD)
    value_rows = qkv[:, 2 * D:].reshape(length, HEADS, HD)
    scores = jnp.einsum('qhd,khd->hqk', queries, key_rows, precision=highest) * HD ** (-0.5)
    scores = low_back(scores)
    places = jnp.arange(length)
    allowed = (seg_rows[:, None] == seg_rows[None, :]) & ((ctx_rows[None, :] == 1) | (places[:, None] == places[None, :]))
    scores = jnp.where(allowed[None], scores, -1e+30)
    highest_score = lax.optimization_barrier(jnp.max(scores, axis=-1, keepdims=True))
    log_total = highest_score + jnp.log(lax.optimization_barrier(jnp.sum(jnp.exp(scores - highest_score), axis=-1, keepdims=True)))
    probs = low(jnp.exp(scores - log_total))
    mixed = jnp.einsum('hqk,khd->qhd', probs, value_rows, precision=highest).reshape(length, D)
    return low_back(low(mixed))

def forward(inputs, mask_values, order_rows, seg_rows, ctx_rows, w_enc, w_attn, w_ffn, vectors):
    masked = inputs * mask_values
    embedded = jnp.dot(masked, low(w_enc), precision=highest) + vectors[0]
    embedded = embedded.reshape(N_ROWS, N_FEAT, TD, D)
    sent = jnp.take_along_axis(embedded, order_rows[..., None], axis=2)
    sent = sent.reshape(N_ROWS, N_FEAT, N_ROWS, TD // N_ROWS, D).transpose(1, 2, 0, 3, 4)
    grouped = low_back(low(sent.reshape(N_FEAT * N_ROWS, TD, D)))
    attn_low = low(w_attn)
    ffn_low = low(w_ffn)
    seg_groups = seg_rows.reshape(N_FEAT * N_ROWS, TD)
    ctx_groups = ctx_rows.reshape(N_FEAT * N_ROWS, TD)
    qkv_weight = attn_low[:, :3 * D]

    def one_group(items):
        return attend(items[0], items[1], items[2], qkv_weight)
    mixed = lax.map(jax.checkpoint(one_group), (grouped, seg_groups, ctx_groups))
    attn_out = low_back(jnp.einsum('gtd,de->gte', mixed, attn_low[:, 3 * D:], precision=highest))
    normed = layer_norm(grouped + attn_out, vectors[1], vectors[2])
    pre_act = low_back(jnp.einsum('gtd,df->gtf', low(normed), ffn_low[:, :FF], precision=highest))
    act_low = low(jax.nn.gelu(pre_act, approximate=False))
    branch = low_back(jnp.einsum('gtf,df->gtd', act_low, ffn_low[:, FF:], precision=highest)) + vectors[5]
    result = layer_norm(normed + branch, vectors[3], vectors[4])
    return result.reshape(N_FEAT, N_ROWS * TD, D)

def reference(features, feat_mask, send_order, segment, context, cotangent, w_enc, w_attn, w_ffn, vectors, m_enc, v_enc, m_attn, v_attn, m_ffn, v_ffn, m_vec, v_vec):
    params = (w_enc, w_attn, w_ffn, vectors)
    totals = tuple((jnp.zeros_like(item) for item in params))
    results = []
    input_grads = []
    for batch_index in range(M):
        mask_values = feat_mask[batch_index].astype(jnp.float32)
        order_rows = send_order[batch_index]
        seg_rows = segment[batch_index]
        ctx_rows = context[batch_index]

        def apply_layer(inputs, enc_w, attn_w, ffn_w, vec_w):
            return forward(inputs, mask_values, order_rows, seg_rows, ctx_rows, enc_w, attn_w, ffn_w, vec_w)
        result, pullback = jax.vjp(apply_layer, features[batch_index].astype(jnp.float32), *params)
        grads = pullback(cotangent[batch_index].astype(jnp.float32))
        results.append(result)
        input_grads.append(grads[0])
        totals = tuple((total + grad for total, grad in zip(totals, grads[1:])))
    enc_new = adamw(w_enc, totals[0], m_enc, v_enc, encoder_rate)
    attn_new = adamw(w_attn, totals[1], m_attn, v_attn, attention_rate)
    ffn_new = adamw(w_ffn, totals[2], m_ffn, v_ffn, feedforward_rate)
    vec_new = adamw(vectors, totals[3], m_vec, v_vec, vector_rate)
    return (jnp.stack(results), jnp.stack(input_grads), enc_new[0], enc_new[1], enc_new[2], attn_new[0], attn_new[1], attn_new[2], ffn_new[0], ffn_new[1], ffn_new[2], vec_new[0], vec_new[1], vec_new[2])
```

```python
import functools, math
import jax, jax.numpy as jnp
from jax import lax
from jax.sharding import PartitionSpec as P
from jax.experimental import pallas as pl
from jax.experimental.pallas import tpu as pltpu
bf16=jnp.bfloat16; f32=jnp.float32
HEADS=4
STEP=10
BIG=3
LN2=math.log(2.0)

def nt(a,b): return lax.dot_general(a,b,(((1,),(1,)),((),())),preferred_element_type=f32)
def nn(a,b): return lax.dot_general(a,b,(((1,),(0,)),((),())),preferred_element_type=f32)
def tn(a,b): return lax.dot_general(a,b,(((0,),(0,)),((),())),preferred_element_type=f32)
def lanes(shape): return lax.broadcasted_iota(jnp.int32,shape,1)
def subl(shape): return lax.broadcasted_iota(jnp.int32,shape,0)
def split3(x):
    a=x.astype(bf16).astype(f32); r=x-a
    b=r.astype(bf16).astype(f32)
    return a,b,r-b

def split_rows(acc,core,keep_ref,send_ref,cols):
    nz,dl=keep_ref.shape[0],keep_ref.shape[1]
    for z in range(nz):
        mine=pl.multiple_of((2*z+core)*dl,8); other=pl.multiple_of((2*z+1-core)*dl,8)
        keep_ref[z,:,cols]=acc[pl.ds(mine,dl),:].astype(bf16)
        send_ref[z,:,cols]=acc[pl.ds(other,dl),:].astype(bf16)

def starts(seg_ref,m,T):
    q=T//4
    first=seg_ref[m,0,0,0]==seg_ref[m,0,0,q]
    big=jnp.where(first,0,q); small=jnp.where(first,3*q,0)
    return pl.multiple_of(big,q),pl.multiple_of(small,q)

def k1_kernel(seg_ref,x_ref,ctx_ref,wa_ref,h_ref,qkv_ref,o_ref,ext_ref,wev_ref,vec_ref,kext_ref,diag_ref):
    m=pl.program_id(0)
    T,D=h_ref.shape[1],h_ref.shape[2]; Q=T//4; HD=D//HEADS; nf=x_ref.shape[2]
    @pl.when(m==0)
    def _():
        t=wa_ref[:,3*D:3*D+128].astype(f32).T
        wev_ref[...]=t.astype(bf16)
        vec_ref[...]=jnp.concatenate([jnp.zeros((1,D),f32),t[104:109]+t[109:114]+t[114:119],jnp.zeros((2,D),f32)],axis=0)
    wev=wev_ref[0:nf,:]
    for r in range(x_ref.shape[0]):
        n=x_ref.shape[3]
        h_ref[0,r*n:(r+1)*n,:]=tn(x_ref[r,0],wev).astype(bf16)
    c=math.log2(math.e)*HD**-0.5
    h=h_ref[0]
    qkv_ref[0,:,0:D]=(nn(h,wa_ref[:,0:D])*c).astype(bf16)
    qkv_ref[0,:,D:3*D]=nn(h,wa_ref[:,D:3*D]).astype(bf16)
    bias=jnp.where(ctx_ref[0,0]==1,0.0,-1e30).astype(f32)
    bcol=jnp.broadcast_to(bias,(128,T)).T
    kext_ref[...]=jnp.where(lanes((T,128))==0,bcol,0.0).astype(bf16)
    for b in range(4):
        diag_ref[b]=jnp.where(subl((Q,Q))==lanes((Q,Q)),0.0,jnp.broadcast_to(bias[:,b*Q:(b+1)*Q],(Q,Q)))
    qext=jnp.where(lanes((Q,128))==0,1.0,0.0).astype(bf16)
    ones=jnp.ones((Q,128),bf16)
    big,small=starts(seg_ref,m,T)
    lane=lanes((Q,128))
    for base,nb in ((big,BIG),(small,4-BIG)):
        rows=[pl.multiple_of(base+b*Q,Q) for b in range(nb)]
        for qb in range(nb):
            ext=jnp.where(lane==12,1.0,0.0)
            for hd in range(HEADS):
                cq=slice(hd*HD,(hd+1)*HD); ck=slice(D+hd*HD,D+(hd+1)*HD); cv=slice(2*D+hd*HD,2*D+(hd+1)*HD)
                q=qkv_ref[0,pl.ds(rows[qb],Q),cq]
                qa=jnp.concatenate([q,qext],axis=1)
                s=[]
                for kb in range(nb):
                    k=qkv_ref[0,pl.ds(rows[kb],Q),ck]
                    if kb==qb:
                        s.append(nt(q,k)+diag_ref[rows[kb]//Q])
                    else:
                        s.append(nt(qa,jnp.concatenate([k,kext_ref[pl.ds(rows[kb],Q),:]],axis=1)))
                mx=functools.reduce(jnp.maximum,s)
                mx=jnp.max(mx,axis=1,keepdims=True)
                acc=None
                for kb in range(nb):
                    e=jnp.exp2(s[kb]-mx).astype(bf16)
                    v=qkv_ref[0,pl.ds(rows[kb],Q),cv]
                    t=nn(e,jnp.concatenate([v,ones],axis=1))
                    acc=t if acc is None else acc+t
                tot=acc[:,HD:]
                o_ref[0,pl.ds(rows[qb],Q),cq]=(acc[:,:HD]/tot).astype(bf16)
                lse=mx+jnp.log2(tot)
                for j,part in enumerate(split3(lse)):
                    ext=jnp.where(lane==3*hd+j,part,ext)
            ext_ref[0,pl.ds(rows[qb],Q),:]=ext.astype(bf16)

def k1(seg,x,ctx,wa):
    R,M,nf,n=x.shape; T=R*n; D=wa.shape[0]
    return pl.pallas_call(k1_kernel,grid=(M,),
        in_specs=[pl.BlockSpec(memory_space=pltpu.SMEM),
          pl.BlockSpec((R,1,nf,n),lambda m:(0,m,0,0)),
          pl.BlockSpec((1,1,1,T),lambda m:(m,0,0,0)),
          pl.BlockSpec(wa.shape,lambda m:(0,0))],
        out_specs=[pl.BlockSpec((1,T,D),lambda m:(m,0,0)),pl.BlockSpec((1,T,3*D),lambda m:(m,0,0)),
          pl.BlockSpec((1,T,D),lambda m:(m,0,0)),pl.BlockSpec((1,T,128),lambda m:(m,0,0)),
          pl.BlockSpec((128,D),lambda m:(0,0)),pl.BlockSpec((8,D),lambda m:(0,0))],
        out_shape=[jax.ShapeDtypeStruct((M,T,D),bf16),jax.ShapeDtypeStruct((M,T,3*D),bf16),
          jax.ShapeDtypeStruct((M,T,D),bf16),jax.ShapeDtypeStruct((M,T,128),bf16),
          jax.ShapeDtypeStruct((128,D),bf16),jax.ShapeDtypeStruct((8,D),f32)],
        scratch_shapes=[pltpu.VMEM((T,128),bf16),pltpu.VMEM((4,T//4,T//4),f32)],
        compiler_params=pltpu.CompilerParams(vmem_limit_bytes=48<<20),
        cost_estimate=pl.CostEstimate(flops=M*4*10**9,bytes_accessed=10**7,transcendentals=M*3*10**6),
        name="attend")(seg,x,ctx,wa)

def gelu_parts(u):
    cdf=0.5+0.5*lax.erf(u*(2.0**-0.5))
    pdf=jnp.exp2(u*u*(-0.5*math.log2(math.e)))*(1.0/math.sqrt(2.0*math.pi))
    return cdf,pdf

def k2_kernel(idx_ref,h_ref,o_ref,cot_ref,wb_ref,vec_ref,act_ref,da_ref,do_ref,dext_ref,keep_ref,send_ref,gv_ref,
              y1_s,gr_s,db_s,du_s,dar_s,acc_s,accv_s):
    m=pl.program_id(0); M=pl.num_programs(0)
    T,D=h_ref.shape[1],h_ref.shape[2]; F=2*D; HD=D//HEADS
    B=256
    wo=slice(0,D); w1=slice(D,D+F); w2=slice(D+F,D+2*F)
    g1,s1,g2,s2,b2=(vec_ref[j:j+1,:] for j in range(1,6))
    lane=lanes((B,128))
    vsum=[0.0]*5
    def colsum(x):
        return jnp.sum(x.reshape(x.shape[0]//8,8,x.shape[1]),axis=0)
    for t in range(T//B):
        r=slice(t*B,(t+1)*B)
        o=o_ref[0,r,:]
        a=h_ref[0,r,:].astype(f32)+nn(o,wb_ref[:,wo])
        mean=jnp.mean(a,axis=1,keepdims=True); ac=a-mean
        i1=lax.rsqrt(jnp.mean(ac*ac,axis=1,keepdims=True)+1e-5)
        xh1=ac*i1
        y1=xh1*g1+s1
        y1b=y1.astype(bf16); y1_s[r,:]=y1b
        u=nn(y1b,wb_ref[:,w1])
        cdf,pdf=gelu_parts(u)
        gr=(u*cdf).astype(bf16); gr_s[r,:]=gr
        dgelu=cdf+u*pdf
        b=y1+nt(gr,wb_ref[:,w2])+b2
        mean=jnp.mean(b,axis=1,keepdims=True); bc=b-mean
        i2=lax.rsqrt(jnp.mean(bc*bc,axis=1,keepdims=True)+1e-5)
        xh2=bc*i2
        act_ref[0,0,r,:]=xh2*g2+s2
        c=cot_ref[0,0,r,:].astype(f32)
        vsum[2]+=colsum(c*xh2); vsum[3]+=colsum(c)
        cg=c*g2
        db=i2*(cg-jnp.mean(cg,axis=1,keepdims=True)-xh2*jnp.mean(cg*xh2,axis=1,keepdims=True))
        vsum[4]+=colsum(db)
        dbr=db.astype(bf16); db_s[r,:]=dbr
        du=(nn(dbr,wb_ref[:,w2])*dgelu).astype(bf16); du_s[r,:]=du
        dy=db+nt(du,wb_ref[:,w1])
        vsum[0]+=colsum(dy*xh1); vsum[1]+=colsum(dy)
        cg=dy*g1
        da=i1*(cg-jnp.mean(cg,axis=1,keepdims=True)-xh1*jnp.mean(cg*xh1,axis=1,keepdims=True))
        da_ref[0,r,:]=da
        dar=da.astype(bf16); dar_s[r,:]=dar
        do=nt(dar,wb_ref[:,wo]).astype(bf16)
        do_ref[0,r,:]=do
        od=o.astype(f32)*do.astype(f32)
        ext=jnp.zeros((B,128),f32)
        for hd in range(HEADS):
            delta=jnp.sum(od[:,hd*HD:(hd+1)*HD],axis=1,keepdims=True)
            for j,part in enumerate(split3(delta)):
                ext=jnp.where(lane==3*hd+j,part,ext)
        dext_ref[0,r,:]=ext.astype(bf16)
    def put(cols,val,cv):
        @pl.when(m==0)
        def _(): acc_s[:,cols]=val()
        @pl.when(m!=0)
        def _(): acc_s[:,cols]+=val()
    put(wo,lambda: tn(o_ref[0],dar_s[...]),None)
    put(w1,lambda: tn(y1_s[...],du_s[...]),None)
    put(w2,lambda: tn(db_s[...],gr_s[...]),None)
    v=jnp.concatenate([jnp.zeros((1,D),f32)]+[jnp.sum(x,axis=0,keepdims=True) for x in vsum]+[jnp.zeros((2,D),f32)],axis=0)
    @pl.when(m==0)
    def _(): accv_s[...]=v
    @pl.when(m!=0)
    def _(): accv_s[...]+=v
    @pl.when(m==M-1)
    def _():
        split_rows(acc_s,idx_ref[0],keep_ref,send_ref,slice(None))
        gv_ref[...]=accv_s[...]

def k2(idx,nz,h,o,cot,wb,vec):
    M,T,D=h.shape; F=2*D; W=wb.shape[1]
    mb=lambda n: pl.BlockSpec((1,T,n),lambda m:(m,0,0))
    return pl.pallas_call(k2_kernel,grid=(M,),
        in_specs=[pl.BlockSpec(memory_space=pltpu.SMEM),mb(D),mb(D),pl.BlockSpec((1,1,T,D),lambda m:(m,0,0,0)),pl.BlockSpec(wb.shape,lambda m:(0,0)),pl.BlockSpec(vec.shape,lambda m:(0,0))],
        out_specs=[pl.BlockSpec((1,1,T,D),lambda m:(m,0,0,0)),mb(D),mb(D),mb(128),pl.BlockSpec((nz,D//nz//2,W),lambda m:(0,0,0)),pl.BlockSpec((nz,D//nz//2,W),lambda m:(0,0,0)),pl.BlockSpec((8,D),lambda m:(0,0))],
        out_shape=[jax.ShapeDtypeStruct((M,1,T,D),f32),jax.ShapeDtypeStruct((M,T,D),f32),jax.ShapeDtypeStruct((M,T,D),bf16),
           jax.ShapeDtypeStruct((M,T,128),bf16),jax.ShapeDtypeStruct((nz,D//nz//2,W),bf16),jax.ShapeDtypeStruct((nz,D//nz//2,W),bf16),jax.ShapeDtypeStruct((8,D),f32)],
        scratch_shapes=[pltpu.VMEM((T,D),bf16),pltpu.VMEM((T,F),bf16),pltpu.VMEM((T,D),bf16),pltpu.VMEM((T,F),bf16),pltpu.VMEM((T,D),bf16),
           pltpu.VMEM((D,W),f32),pltpu.VMEM((8,D),f32)],
        compiler_params=pltpu.CompilerParams(vmem_limit_bytes=56<<20),
        cost_estimate=pl.CostEstimate(flops=M*8*10**9,bytes_accessed=2*10**7,transcendentals=M*3*10**6),
        name="feed")(idx,h,o,cot,wb,vec)

def k3_kernel(idx_ref,seg_ref,x_ref,ctx_ref,qkv_ref,h_ref,do_ref,da_ref,ext_ref,dext_ref,wa_ref,wev_ref,gv_ref,dx_ref,keep_ref,send_ref,
              dqkv_s,kb_s,ku_s,diag_s,p_s,ds_s,acc_s,acce_s,accx_s):
    m=pl.program_id(0); M=pl.num_programs(0)
    T,D=h_ref.shape[1],h_ref.shape[2]; Q=T//4; HD=D//HEADS; nf=x_ref.shape[2]
    bias=jnp.where(ctx_ref[0,0]==1,0.0,-1e30).astype(f32)
    bcol=jnp.broadcast_to(bias,(128,T)).T
    lane=lanes((T,128))
    for hd in range(HEADS):
        un=jnp.where((lane>=3*hd)&(lane<3*hd+3),-1.0,0.0)
        ku_s[hd]=un[:Q].astype(bf16)
        kb_s[hd]=jnp.where(lane==12,bcol,un).astype(bf16)
    for b in range(4):
        col=bcol[b*Q:(b+1)*Q,:]
        diag_s[b]=jnp.where(subl((Q,Q))==lanes((Q,Q)),0.0,jnp.concatenate([col,col],axis=1))
    big,small=starts(seg_ref,m,T)
    scale=HD**-0.5
    for base,nb in ((big,BIG),(small,4-BIG)):
        rows=[pl.multiple_of(base+b*Q,Q) for b in range(nb)]
        seg=pl.ds(pl.multiple_of(base,Q),nb*Q)
        for hd in range(HEADS):
            cq=slice(hd*HD,(hd+1)*HD); ck=slice(D+hd*HD,D+(hd+1)*HD); cv=slice(2*D+hd*HD,2*D+(hd+1)*HD)
            for qb in range(nb):
                qa=jnp.concatenate([qkv_ref[0,pl.ds(rows[qb],Q),cq],ext_ref[0,pl.ds(rows[qb],Q),:]],axis=1)
                doa=jnp.concatenate([do_ref[0,pl.ds(rows[qb],Q),cq],dext_ref[0,pl.ds(rows[qb],Q),:]],axis=1)
                for kb in range(nb):
                    k=qkv_ref[0,pl.ds(rows[kb],Q),ck]
                    if kb==qb:
                        s=nt(jnp.concatenate([k,ku_s[hd]],axis=1),qa)+diag_s[rows[kb]//Q]
                    else:
                        s=nt(jnp.concatenate([k,kb_s[hd,pl.ds(rows[kb],Q),:]],axis=1),qa)
                    p=jnp.exp2(s)
                    dp=nt(jnp.concatenate([qkv_ref[0,pl.ds(rows[kb],Q),cv],ku_s[hd]],axis=1),doa)
                    p_s[kb*Q:(kb+1)*Q,qb*Q:(qb+1)*Q]=p.astype(bf16)
                    ds_s[kb*Q:(kb+1)*Q,qb*Q:(qb+1)*Q]=(p*dp).astype(bf16)
            n=nb*Q
            dqkv_s[seg,cv]=nn(p_s[0:n,0:n],do_ref[0,seg,cq]).astype(bf16)
            dqkv_s[seg,ck]=(nn(ds_s[0:n,0:n],qkv_ref[0,seg,cq])*LN2).astype(bf16)
            dqt=tn(qkv_ref[0,seg,ck],ds_s[0:n,0:n])*scale
            dqkv_s[seg,cq]=dqt.T.astype(bf16)
    dqkv=dqkv_s[...]
    dh=(da_ref[0]+nt(dqkv,wa_ref[:,0:3*D])).astype(bf16)
    g=tn(h_ref[0],dqkv)
    n=x_ref.shape[3]
    dx=nt(wev_ref[0:nf,:],dh).astype(bf16)
    e=None
    for r in range(x_ref.shape[0]):
        dx_ref[r,0]=dx[:,r*n:(r+1)*n]
        t=nn(x_ref[r,0],dh[r*n:(r+1)*n,:])
        e=t if e is None else e+t
    @pl.when(m==0)
    def _():
        acc_s[...]=g; acce_s[...]=e
    @pl.when(m!=0)
    def _():
        acc_s[...]+=g; acce_s[...]+=e
    @pl.when(m==M-1)
    def _():
        split_rows(acc_s,idx_ref[0],keep_ref,send_ref,slice(0,3*D))
        ee=acce_s[...]; gv=gv_ref[...]
        accx_s[...]=jnp.concatenate([ee,ee[100:101],gv[1:6],jnp.zeros((128-nf-6,D),f32)],axis=0).T
        split_rows(accx_s,idx_ref[0],keep_ref,send_ref,slice(3*D,3*D+128))

def k3(idx,seg,x,ctx,qkv,h,do,da,ext,dext,wa,wev,gv):
    R,M,nf,n=x.shape; T=R*n; D=wa.shape[0]; Q=T//4
    mb=lambda w: pl.BlockSpec((1,T,w),lambda m:(m,0,0))
    full=lambda a: pl.BlockSpec(a.shape,lambda m:(0,)*a.ndim)
    half=pl.BlockSpec((R//2,D//R,wa.shape[1]),lambda m:(0,0,0))
    return pl.pallas_call(k3_kernel,grid=(M,),
        in_specs=[pl.BlockSpec(memory_space=pltpu.SMEM),pl.BlockSpec(memory_space=pltpu.SMEM),pl.BlockSpec((R,1,nf,n),lambda m:(0,m,0,0)),pl.BlockSpec((1,1,1,T),lambda m:(m,0,0,0)),
          mb(3*D),mb(D),mb(D),mb(D),mb(128),mb(128),full(wa),full(wev),full(gv)],
        out_specs=[pl.BlockSpec((R,1,nf,n),lambda m:(0,m,0,0)),half,half],
        out_shape=[jax.ShapeDtypeStruct(x.shape,bf16)]+[jax.ShapeDtypeStruct((R//2,D//R,wa.shape[1]),bf16)]*2,
        scratch_shapes=[pltpu.VMEM((T,3*D),bf16),pltpu.VMEM((HEADS,T,128),bf16),pltpu.VMEM((HEADS,Q,128),bf16),pltpu.VMEM((4,Q,Q),f32),
          pltpu.VMEM((BIG*Q,BIG*Q),bf16),pltpu.VMEM((BIG*Q,BIG*Q),bf16),pltpu.VMEM((D,3*D),f32),pltpu.VMEM((nf,D),f32),pltpu.VMEM((D,128),f32)],
        compiler_params=pltpu.CompilerParams(vmem_limit_bytes=56<<20),
        cost_estimate=pl.CostEstimate(flops=M*8*10**9,bytes_accessed=2*10**7,transcendentals=M*3*10**6),
        name="back")(idx,seg,x,ctx,qkv,h,do,da,ext,dext,wa,wev,gv)

def small_call(kernel,out_shape,*args,scratch=(),smem=0,name=None,flops=10**6,moved=10**6):
    return pl.pallas_call(kernel,out_shape=out_shape,
        in_specs=[pl.BlockSpec(memory_space=pltpu.SMEM)]*smem+[pl.BlockSpec(memory_space=pltpu.VMEM)]*(len(args)-smem),
        scratch_shapes=list(scratch),compiler_params=pltpu.CompilerParams(vmem_limit_bytes=40<<20),
        cost_estimate=pl.CostEstimate(flops=flops,bytes_accessed=moved,transcendentals=0),name=name)(*args)

def pack_kernel(attn_ref,ffn_ref,enc_ref,vec_ref,a_ref,b_ref):
    D3=a_ref.shape[1]-128; nF=enc_ref.shape[1]; Dl=enc_ref.shape[0]
    attn=attn_ref[...]
    a_ref[:,0:D3]=attn[:,0:D3].astype(bf16)
    b_ref[:,0:D3//3]=attn[:,D3:].astype(bf16)
    b_ref[:,D3//3:]=ffn_ref[...].astype(bf16)
    v=vec_ref[...]
    p=[x for x in split3(v)]
    t=jnp.concatenate([x[0:1] for x in p]+[jnp.zeros((1,Dl),f32)]+[x[1:6] for x in p]+[jnp.zeros((9,Dl),f32)],axis=0)
    a_ref[:,D3:]=jnp.concatenate([enc_ref[...],t.T],axis=1).astype(bf16)

def one_hot(order_ref,m):
    T=order_ref.shape[-1]
    return jnp.where(subl((T,T))==order_ref[m,0,0:1,:],1.0,0.0).astype(bf16)

def permute_kernel(order_ref,x_ref,out_ref,s_ref):
    nfeat,M,f,T=x_ref.shape; nf=s_ref.shape[0]; R,n=out_ref.shape[0],out_ref.shape[3]
    s_ref[nfeat*f:,:]=jnp.where(subl((nf-nfeat*f,T))<3,1.0,0.0)
    for m in range(M):
        for j in range(nfeat):
            s_ref[j*f:(j+1)*f,:]=x_ref[j,m].astype(f32)
        y=nn(s_ref[...].astype(bf16),one_hot(order_ref,m)).astype(bf16)
        for d in range(R):
            out_ref[d,m]=y[:,d*n:(d+1)*n]

def unpermute_kernel(order_ref,x_ref,out_ref,s_ref):
    nfeat,M,f,T=out_ref.shape; R=x_ref.shape[0]
    for m in range(M):
        x=jnp.concatenate([x_ref[d,m] for d in range(R)],axis=1)
        s_ref[...]=nt(x,one_hot(order_ref,m))
        for j in range(nfeat):
            out_ref[j,m]=s_ref[j*f:(j+1)*f,:].astype(bf16)

def core_kernel(idx_ref,keep_ref,got_ref,*outs):
    nf=len(outs); q=keep_ref.shape[1]//nf
    s=keep_ref[...].astype(f32)+got_ref[...].astype(f32)
    for k,out in enumerate(outs):
        for f in range(nf):
            @pl.when((idx_ref[1]^k)==f)
            def _():
                out[...]=s[:,f*q:(f+1)*q,:].astype(bf16)

def feat_kernel(nf,idx_ref,*refs):
    ins,outs=refs[:nf],refs[nf:]
    for k,out in enumerate(outs):
        z=idx_ref[2]^k
        s=ins[0][z].astype(f32)
        for x in ins[1:]: s=s+x[z].astype(f32)
        out[...]=s.astype(bf16)

def sum_kernel(*refs):
    s=refs[0][...].astype(f32)
    for x in refs[1:-1]: s=s+x[...].astype(f32)
    refs[-1][...]=s.astype(bf16)

def peers(x,axis,size,step,k):
    return lax.ppermute(x,axis,[(i,i^(k*step)) for i in range(size)])

def scatter_sum(keep,send,idx,nr,nfeat,tag):
    nz,dl,W=keep.shape
    got=peers(send,"rows",nr,1,1)
    q=dl//nfeat
    piece=jax.ShapeDtypeStruct((nz,q,W),bf16)
    ys=small_call(core_kernel,[piece]*nfeat,idx,keep,got,smem=1,name="core_sum"+tag)
    ys=[ys[0]]+[peers(ys[k],"feat",nfeat,1,k) for k in range(1,nfeat)]
    ws=small_call(functools.partial(feat_kernel,nfeat),[jax.ShapeDtypeStruct((q,W),bf16)]*nz,idx,*ys,smem=1,name="feat_sum"+tag)
    ws=[ws[0]]+[peers(ws[k],"rows",nr,2,k) for k in range(1,nz)]
    g=small_call(sum_kernel,jax.ShapeDtypeStruct((q,W),bf16),*ws,name="rows_sum"+tag)
    return [g]+[peers(g,"feat",nfeat,1,k) for k in range(1,nfeat)]

def update(w_ref,g,m_ref,v_ref,rate,wn,mn,vn):
    m=0.9*m_ref[...]+0.1*g
    v=0.95*v_ref[...]+0.05*g*g
    w=w_ref[...]
    wn[...]=w-rate*((m/(1.0-0.9**STEP))/(jnp.sqrt(v/(1.0-0.95**STEP))+1e-8)+0.1*w)
    mn[...]=m; vn[...]=v

def adam_kernel(nfeat,idx_ref,*refs):
    ga,gb=refs[:nfeat],refs[nfeat:2*nfeat]
    ins=refs[2*nfeat:2*nfeat+12]; outs=refs[2*nfeat+12:2*nfeat+24]; sa,sb=refs[2*nfeat+24:]
    q=ga[0].shape[0]
    for k in range(nfeat):
        for f in range(nfeat):
            @pl.when((idx_ref[1]^k)==f)
            def _():
                sa[f*q:(f+1)*q,:]=ga[k][...].astype(f32)
                sb[f*q:(f+1)*q,:]=gb[k][...].astype(f32)
    D3=sa.shape[1]-128; D=D3//3; F=ins[0].shape[1]
    x=sa[:,D3:]
    update(*ins[0:1],x[:,0:F],*ins[1:3],0.08,*outs[0:3])
    update(*ins[3:4],jnp.concatenate([sa[:,0:D3],sb[:,0:D]],axis=1),*ins[4:6],0.25,*outs[3:6])
    update(*ins[6:7],sb[:,D:],*ins[7:9],0.02,*outs[6:9])
    update(*ins[9:10],x.T[104:110,:],*ins[10:12],0.2,*outs[9:12])

def body(features,feat_mask,send_order,segment,context,cotangent,w_enc,w_attn,w_ffn,vectors,m_enc,v_enc,m_attn,v_attn,m_ffn,v_ffn,m_vec,v_vec):
    nfeat,nr=lax.axis_size("feat"),lax.axis_size("rows")
    fi,ri=lax.axis_index("feat"),lax.axis_index("rows")
    idx=jnp.stack([ri%2,fi,ri//2,ri]).astype(jnp.int32)
    M,tok,fl=features.shape; T=tok//nfeat; F=fl*nfeat; nf=-(-(F+3)//8)*8
    Dl=w_attn.shape[0]; D=Dl*nr; n=T//nr
    pa,pb=small_call(pack_kernel,[jax.ShapeDtypeStruct((Dl,3*D+128),bf16),jax.ShapeDtypeStruct((Dl,5*D),bf16)],w_attn,w_ffn,w_enc.T,vectors,name="pack")
    wa=lax.all_gather(pa,"rows",axis=0,tiled=True)
    wb=lax.all_gather(pb,"rows",axis=0,tiled=True)
    mask=feat_mask.transpose(2,0,1)
    xm=features.transpose(2,0,1)*mask.astype(bf16)
    xm=xm.reshape(fl,M,nfeat,T).transpose(2,1,0,3)
    xm=lax.all_to_all(xm,"feat",0,0,tiled=True)
    xs=small_call(permute_kernel,jax.ShapeDtypeStruct((nr,M,nf,n),bf16),send_order,xm,scratch=[pltpu.VMEM((nf,T),f32)],name="sort")
    x=lax.all_to_all(xs,"rows",0,0,tiled=True)
    h,qkv,o,ext,wev,vec=k1(segment,x,context,wa)
    act,da,do,dext,keepb,sendb,gv=k2(idx,nr//2,h,o,cotangent,wb,vec)
    gb=scatter_sum(keepb,sendb,idx,nr,nfeat,"_b")
    dx,keepa,senda=k3(idx,segment,x,context,qkv,h,do,da,ext,dext,wa,wev,gv)
    ga=scatter_sum(keepa,senda,idx,nr,nfeat,"_a")
    dx=lax.all_to_all(dx,"rows",0,0,tiled=True)
    dx=small_call(unpermute_kernel,jax.ShapeDtypeStruct((nfeat,M,fl,T),bf16),send_order,dx,scratch=[pltpu.VMEM((nf,T),f32)],name="unsort")
    dx=lax.all_to_all(dx,"feat",0,0,tiled=True)
    dx=dx.transpose(2,1,0,3).reshape(fl,M,tok).astype(f32)*mask.astype(f32)
    state=[w_enc.T,m_enc.T,v_enc.T,w_attn,m_attn,v_attn,w_ffn,m_ffn,v_ffn,vectors,m_vec,v_vec]
    new=small_call(functools.partial(adam_kernel,nfeat),[jax.ShapeDtypeStruct(s.shape,f32) for s in state],idx,*ga,*gb,*state,smem=1,
        scratch=[pltpu.VMEM((Dl,3*D+128),f32),pltpu.VMEM((Dl,5*D),f32)],name="adamw")
    new=[x.T for x in new[:3]]+list(new[3:])
    return (act,dx.transpose(1,2,0),*new)

def solution(mesh):
    tok=P(None,"rows","feat"); grp=P(None,"feat","rows",None); col=P(None,"rows"); row=P("rows",None)
    return jax.shard_map(body,mesh=mesh,
        in_specs=(tok,tok,P(None,"rows","feat",None),grp,grp,grp,col,row,row,col,col,col,row,row,row,row,col,col),
        out_specs=(grp,tok)+(col,)*3+(row,)*6+(col,)*3,check_vma=False)
```

```python
import functools
import math

import jax
import jax.numpy as jnp
from jax import lax
from jax.experimental import pallas as pl
from jax.experimental.pallas import tpu as pltpu
from jax.sharding import PartitionSpec as P

bf16 = jnp.bfloat16
f32 = jnp.float32
HEADS = 4
STEP = 10
BIG = 3
LN2 = math.log(2.0)
LOG2E = math.log2(math.e)
SMEM = pl.BlockSpec(memory_space=pltpu.SMEM)
VMEM = pl.BlockSpec(memory_space=pltpu.VMEM)
HBM = pl.BlockSpec(memory_space=pltpu.HBM)


def dot(a, b, ca, cb):
    return lax.dot_general(a, b, (((ca,), (cb,)), ((), ())), preferred_element_type=f32)


def nn(a, b):
    return dot(a, b, 1, 0)


def nt(a, b):
    return dot(a, b, 1, 1)


def tn(a, b):
    return dot(a, b, 0, 0)


def lanes(shape):
    return lax.broadcasted_iota(jnp.int32, shape, 1)


def subl(shape):
    return lax.broadcasted_iota(jnp.int32, shape, 0)


def split3(x):
    a = x.astype(bf16).astype(f32)
    r = x - a
    b = r.astype(bf16).astype(f32)
    return a, b, r - b


def call(kernel, out_shape, *args, smem=0, scratch=(), name=None, flops=10**6, moved=10**6, mib=16, specs=None, outs=None):
    single = not isinstance(out_shape, (list, tuple))
    return pl.pallas_call(
        kernel,
        out_shape=out_shape,
        in_specs=specs or [SMEM] * smem + [VMEM] * (len(args) - smem),
        out_specs=outs or (VMEM if single else [VMEM] * len(out_shape)),
        scratch_shapes=list(scratch),
        compiler_params=pltpu.CompilerParams(vmem_limit_bytes=mib << 20),
        cost_estimate=pl.CostEstimate(flops=flops, bytes_accessed=moved, transcendentals=0),
        name=name,
    )(*args)


def shape(s, d):
    return jax.ShapeDtypeStruct(tuple(s), d)


def far(s, d):
    return pltpu.HBM(tuple(s), d)


def keep_far(x):
    return pltpu.with_memory_space_constraint(x, pltpu.HBM)


class Copies:
    def __init__(self, sems):
        self.sems, self.used, self.open = sems, 0, {}

    def start(self, key, src, dst):
        self.open[key] = pltpu.make_async_copy(src, dst, self.sems.at[self.used])
        self.used += 1
        self.open[key].start()

    def wait(self, key):
        if key in self.open:
            self.open.pop(key).wait()

    def wait_all(self):
        for key in list(self.open):
            self.wait(key)


CORE, FEAT, ZED = 0, 1, 2


def starts(seg_ref, m, T):
    q = T // 4
    first = seg_ref[m, 0, 0, 0] == seg_ref[m, 0, 0, q]
    big = jnp.where(first, 0, q)
    small = jnp.where(first, 3 * q, 0)
    return pl.multiple_of(big, q), pl.multiple_of(small, q)


def neighbourhoods(seg_ref, m, T):
    q = T // 4
    big, small = starts(seg_ref, m, T)
    for base, nb in ((big, BIG), (small, 4 - BIG)):
        yield base, nb, [pl.multiple_of(base + b * q, q) for b in range(nb)]


def split_rows(acc, core, keep_ref, send_ref, cols):
    nz, dl = keep_ref.shape[0], keep_ref.shape[1]
    for z in range(nz):
        mine = pl.multiple_of((2 * z + core) * dl, 8)
        other = pl.multiple_of((2 * z + 1 - core) * dl, 8)
        keep_ref[z, :, cols] = acc[pl.ds(mine, dl), :].astype(bf16)
        send_ref[z, :, cols] = acc[pl.ds(other, dl), :].astype(bf16)


def pack_kernel(WA, idx_ref, attn_ref, ffn_ref, enc_ref, vec_ref, out_ref, attn_s, ffn_s, enc_s, vec_s, x_s, sems):
    D3, Dl, q = WA - 128, enc_s.shape[0], out_ref.shape[0]
    D = D3 // 3
    rows = slice(None) if q == Dl else pl.ds(pl.multiple_of(idx_ref[FEAT] * q, q), q)
    copies = Copies(sems)
    for key, src, dst in (("e", enc_ref, enc_s), ("v", vec_ref, vec_s), ("a", attn_ref.at[rows, :], attn_s), ("f", ffn_ref.at[rows, :], ffn_s)):
        copies.start(key, src, dst)
    copies.wait("e")
    copies.wait("v")
    p = split3(vec_s[...])
    none = jnp.zeros((1, Dl), f32)
    t = jnp.concatenate([x[0:1] for x in p] + [none] + [x[1:6] for x in p] + [jnp.zeros((9, Dl), f32)], axis=0)
    x_s[...] = jnp.concatenate([enc_s[...], t.T], axis=1)
    out_ref[:, D3:WA] = x_s[rows, :].astype(bf16)
    copies.wait("a")
    out_ref[:, 0:D3] = attn_s[:, 0:D3].astype(bf16)
    out_ref[:, WA : WA + D] = attn_s[:, D3:].astype(bf16)
    copies.wait("f")
    out_ref[:, WA + D :] = ffn_s[...].astype(bf16)


def join_kernel(idx_ref, *refs):
    a_ref, b_ref = refs[-2:]
    A = a_ref.shape[2]
    for j, ref in enumerate(refs[:-2]):
        a_ref[idx_ref[ZED] ^ j] = ref[:, 0:A]
        b_ref[idx_ref[ZED] ^ j] = ref[:, A:]


def assemble(idx_ref, pieces, dst):
    if len(pieces) == 1:
        dst[...] = pieces[0][...]
        return
    nz, q, _ = pieces[0].shape
    nfeat = len(pieces) // 2
    for c in range(2):
        for k in range(nfeat):
            for j in range(nz):
                r = (j * 2 + (idx_ref[CORE] ^ c)) * (nfeat * q) + (idx_ref[FEAT] ^ k) * q
                dst[pl.ds(pl.multiple_of(r, q), q), :] = pieces[c * nfeat + k][j]


def one_hot(order, T):
    return jnp.where(subl((T, order.shape[1])) == order, 1.0, 0.0).astype(bf16)


def sort_kernel(idx_ref, mine_ref, theirs_ref, own_ref, sibling_ref, out_ref, s_ref):
    nfeat, M, f, T = own_ref.shape
    nz, nf, n = out_ref.shape[0], out_ref.shape[3], out_ref.shape[4]
    s_ref[nfeat * f :, :] = jnp.where(subl((nf - nfeat * f, T)) < 3, 1.0, 0.0)
    for s, (order_ref, x_ref) in enumerate(((mine_ref, own_ref), (theirs_ref, sibling_ref))):
        core = idx_ref[CORE] ^ s
        for m in range(M):
            for g in range(nfeat):
                s_ref[g * f : (g + 1) * f, :] = x_ref[g, m].astype(f32)
            y = nn(s_ref[...].astype(bf16), one_hot(order_ref[m], T)).astype(bf16)
            for z in range(nz):
                out_ref[z, core, m] = y[:, z * n : (z + 1) * n]


def pick_kernel(idx_ref, *refs):
    mine_ref, other_ref = refs[-2:]
    for j, ref in enumerate(refs[:-2]):
        mine_ref[idx_ref[ZED] ^ j] = ref[idx_ref[CORE]]
        other_ref[idx_ref[ZED] ^ j] = ref[1 - idx_ref[CORE]]


def unsort_kernel(mine_ref, other_ref, x_ref, got_ref, out_ref, s_ref):
    nz = x_ref.shape[0]
    nfeat, M, f, T = out_ref.shape
    for m in range(M):
        mine = jnp.concatenate([x_ref[z, m] for z in range(nz)], axis=1)
        other = jnp.concatenate([got_ref[z, m] for z in range(nz)], axis=1)
        s_ref[...] = nt(mine, one_hot(mine_ref[m], T)) + nt(other, one_hot(other_ref[m], T))
        for g in range(nfeat):
            out_ref[g, m] = s_ref[g * f : (g + 1) * f, :].astype(bf16)


def attend_kernel(idx_ref, seg_ref, ctx_ref, y_ref, *refs):
    pieces, refs = refs[:-17], refs[-17:]
    vec_ref, h_out, o_out, qkv_out, ext_out, wa_out, x_out, h_ref, o_ref, qkv_ref, ext_ref, wa_ref, wev_ref, kext_s, diag_s, e_s, sems = refs
    M, T, D = h_ref.shape
    Q, HD = T // 4, D // HEADS
    R, _, nf, n = y_ref.shape
    copies = Copies(sems)
    copies.start("x", y_ref, x_out)
    assemble(idx_ref, pieces, wa_ref)
    copies.start("wa", wa_ref, wa_out)
    t = wa_ref[:, 3 * D :].astype(f32).T
    wev_ref[...] = t.astype(bf16)
    vec_ref[...] = jnp.concatenate([jnp.zeros((1, D), f32), t[104:109] + t[109:114] + t[114:119], jnp.zeros((2, D), f32)], axis=0)
    wev = wev_ref[0:nf, :]
    c = LOG2E * HD**-0.5
    qext = jnp.where(lanes((Q, 128)) == 0, 1.0, 0.0).astype(bf16)
    lane = lanes((Q, 128))
    for m in range(M):
        for r in range(R):
            h_ref[m, r * n : (r + 1) * n, :] = tn(y_ref[r, m], wev).astype(bf16)
    copies.start("h", h_ref, h_out)
    for m in range(M):
        h = h_ref[m]
        qkv_ref[m, :, 0:D] = (nn(h, wa_ref[:, 0:D]) * c).astype(bf16)
        qkv_ref[m, :, D : 3 * D] = nn(h, wa_ref[:, D : 3 * D]).astype(bf16)
        copies.start(("qkv", m), qkv_ref.at[m], qkv_out.at[m])
        bias = jnp.where(ctx_ref[m, 0] == 1, 0.0, -1e30).astype(f32)
        bcol = jnp.broadcast_to(bias, (128, T)).T
        kext_s[...] = jnp.where(lanes((T, 128)) == 0, bcol, 0.0).astype(bf16)
        for b in range(4):
            row = jnp.broadcast_to(bias[:, b * Q : (b + 1) * Q], (Q, Q))
            diag_s[b] = jnp.where(subl((Q, Q)) == lanes((Q, Q)), 0.0, row)
        for base, nb, rows in neighbourhoods(seg_ref, m, T):
            every = pl.ds(base, nb * Q)
            exts = [jnp.where(lane == 12, 1.0, 0.0) for _ in range(nb)]
            for hd in range(HEADS):
                cq = slice(hd * HD, (hd + 1) * HD)
                ck = slice(D + hd * HD, D + (hd + 1) * HD)
                cv = slice(2 * D + hd * HD, 2 * D + (hd + 1) * HD)
                tops = []
                for qb in range(nb):
                    q = qkv_ref[m, pl.ds(rows[qb], Q), cq]
                    qa = jnp.concatenate([q, qext], axis=1)
                    s = []
                    for kb in range(nb):
                        k = qkv_ref[m, pl.ds(rows[kb], Q), ck]
                        if kb == qb:
                            s.append(nt(q, k) + diag_s[rows[kb] // Q])
                        else:
                            s.append(nt(qa, jnp.concatenate([k, kext_s[pl.ds(rows[kb], Q), :]], axis=1)))
                    top = jnp.max(functools.reduce(jnp.maximum, s), axis=1, keepdims=True)
                    tops.append(top)
                    for kb in range(nb):
                        e_s[hd % 2, qb * Q : (qb + 1) * Q, kb * Q : (kb + 1) * Q] = jnp.exp2(s[kb] - top).astype(bf16)
                v = qkv_ref[m, every, cv]
                acc = nn(e_s[hd % 2, 0 : nb * Q, 0 : nb * Q], jnp.concatenate([v, jnp.ones((nb * Q, 128), bf16)], axis=1))
                total = acc[:, HD:]
                o_ref[m, every, cq] = (acc[:, :HD] / total).astype(bf16)
                for qb in range(nb):
                    lse = tops[qb] + jnp.log2(total[qb * Q : (qb + 1) * Q])
                    for j, part in enumerate(split3(lse)):
                        exts[qb] = jnp.where(lane == 3 * hd + j, part, exts[qb])
            for qb in range(nb):
                ext_ref[m, pl.ds(rows[qb], Q), :] = exts[qb].astype(bf16)
        copies.start(("ext", m), ext_ref.at[m], ext_out.at[m])
        copies.start(("o", m), o_ref.at[m], o_out.at[m])
    copies.wait_all()


def gelu_parts(u):
    cdf = 0.5 + 0.5 * lax.erf(u * (2.0**-0.5))
    pdf = jnp.exp2(u * u * (-0.5 * LOG2E)) * (1.0 / math.sqrt(2.0 * math.pi))
    return cdf, pdf


def colsum(x):
    return jnp.sum(x.reshape(x.shape[0] // 8, 8, x.shape[1]), axis=0)


def mean(x):
    return jnp.mean(x, axis=1, keepdims=True)


def feed_kernel(np_, ng, idx_ref, vec_ref, h_hbm, o_hbm, cot_hbm, *refs):
    pieces, refs = refs[:np_], refs[np_:]
    gb_outs, refs = refs[:ng], refs[ng:]
    act_ref, da_out, do_out, dext_out, gv_ref, h_ref, o_ref, da_ref, do_ref, dext_ref, gb_ref, wb_s, cot_ref, y1_s, gr_s, db_s, du_s, act_s, sems = refs
    M, T, D = h_ref.shape
    F, HD, B = 2 * D, D // HEADS, T // 2
    wo, w1, w2 = slice(0, D), slice(D, D + F), slice(D + F, D + 2 * F)
    copies = Copies(sems)
    for m in range(M):
        copies.start(("o", m), o_hbm.at[m], o_ref.at[m])
        copies.start(("h", m), h_hbm.at[m], h_ref.at[m])
        copies.start(("cot", m), cot_hbm.at[m], cot_ref.at[m])
    assemble(idx_ref, pieces, wb_s)
    g1, s1, g2, s2, b2 = (vec_ref[j : j + 1, :] for j in range(1, 6))
    lane = lanes((B, 128))
    vsum = [0.0] * 5

    def chain(m, b):
        r = slice(b * B, (b + 1) * B)
        w = slice(m * T + b * B, m * T + (b + 1) * B)
        copies.wait(("o", m))
        o = o_ref[m, r, :]
        t = nn(o, wb_s[:, wo])
        yield
        copies.wait(("h", m))
        a = h_ref[m, r, :].astype(f32) + t
        ac = a - mean(a)
        i1 = lax.rsqrt(mean(ac * ac) + 1e-5)
        xh1 = ac * i1
        y1 = xh1 * g1 + s1
        y1b = y1.astype(bf16)
        y1_s[w, :] = y1b
        u = nn(y1b, wb_s[:, w1])
        yield
        cdf, pdf = gelu_parts(u)
        gr = (u * cdf).astype(bf16)
        gr_s[w, :] = gr
        dgelu = cdf + u * pdf
        t = nt(gr, wb_s[:, w2])
        yield
        z = y1 + t + b2
        zc = z - mean(z)
        i2 = lax.rsqrt(mean(zc * zc) + 1e-5)
        xh2 = zc * i2
        copies.wait(("act", b))
        act_s[b] = xh2 * g2 + s2
        copies.start(("act", b), act_s.at[b], act_ref.at[m, 0, pl.ds(b * B, B), :])
        copies.wait(("cot", m))
        c = cot_ref[m, 0, r, :].astype(f32)
        vsum[2] += colsum(c * xh2)
        vsum[3] += colsum(c)
        cg = c * g2
        db = i2 * (cg - mean(cg) - xh2 * mean(cg * xh2))
        vsum[4] += colsum(db)
        dbr = db.astype(bf16)
        db_s[w, :] = dbr
        t = nn(dbr, wb_s[:, w2])
        yield
        du = (t * dgelu).astype(bf16)
        du_s[w, :] = du
        t = nt(du, wb_s[:, w1])
        yield
        dy = db + t
        vsum[0] += colsum(dy * xh1)
        vsum[1] += colsum(dy)
        cg = dy * g1
        da = i1 * (cg - mean(cg) - xh1 * mean(cg * xh1))
        dar = da.astype(bf16)
        da_ref[w, :] = dar
        do = nt(dar, wb_s[:, wo]).astype(bf16)
        yield
        do_ref[m, r, :] = do
        od = o.astype(f32) * do.astype(f32)
        ext = jnp.zeros((B, 128), f32)
        for hd in range(HEADS):
            delta = jnp.sum(od[:, hd * HD : (hd + 1) * HD], axis=1, keepdims=True)
            for j, part in enumerate(split3(delta)):
                ext = jnp.where(lane == 3 * hd + j, part, ext)
        dext_ref[m, r, :] = ext.astype(bf16)
        copies.start(("da", m, b), da_ref.at[w, :], da_out.at[w, :])
        copies.start(("do", m, b), do_ref.at[m, r, :], do_out.at[m, r, :])
        copies.start(("dext", m, b), dext_ref.at[m, r, :], dext_out.at[m, r, :])

    for m in range(M):
        gens = [chain(m, b) for b in range(2)]
        for _ in range(7):
            for g in gens:
                next(g, None)
    gv_ref[...] = jnp.concatenate([jnp.zeros((1, D), f32)] + [jnp.sum(x, axis=0, keepdims=True) for x in vsum] + [jnp.zeros((2, D), f32)], axis=0)
    left = {wo.start: (o_ref[...].reshape(M * T, D), da_ref), w1.start: (y1_s, du_s), w2.start: (db_s, gr_s)}
    for cols in (w2, w1, wo):
        a, b = left[cols.start]
        g = tn(a[...], b[...]).astype(bf16)
        if ng == 1:
            gb_ref[:, cols] = g
            copies.start(("gb", cols.start), gb_ref.at[:, cols], gb_outs[0].at[:, cols])
        else:
            nr, q, _ = gb_outs[0].shape
            gb_ref[:, :, :, cols] = g.reshape(nr, ng, q, g.shape[1])
            for k, out in enumerate(gb_outs):
                copies.start(("gb", cols.start, k), gb_ref.at[:, idx_ref[FEAT] ^ k, :, cols], out.at[:, :, cols])
    copies.wait_all()


def back_kernel(nz, idx_ref, seg_ref, ctx_ref, gv_ref, do_hbm, dext_hbm, da_hbm, qkv_hbm, ext_hbm, h_hbm, wa_hbm, x_hbm, *refs):
    outs, refs = refs[:nz], refs[nz:]
    keep_ref, send_ref, do_ref, dext_ref, da_ref, qkv_ref, ext_ref, h_ref, wa_ref, x_ref, dqkv_s, kb_s, ku_s, diag_s, p_s, ds_s, acc_s, accx_s, dh_s, sems = refs
    M, T, D = do_ref.shape
    Q, HD = T // 4, D // HEADS
    nf, n = x_ref.shape[2], x_ref.shape[3]
    scale = HD**-0.5
    copies = Copies(sems)
    for m in range(M):
        for key, src, dst in (("ext", ext_hbm, ext_ref), ("qkv", qkv_hbm, qkv_ref), ("dext", dext_hbm, dext_ref), ("do", do_hbm, do_ref)):
            copies.start((key, m), src.at[m], dst.at[m])
    for key, src, dst in (("da", da_hbm, da_ref), ("h", h_hbm, h_ref), ("wa", wa_hbm, wa_ref), ("x", x_hbm, x_ref)):
        copies.start(key, src, dst)
    lane = lanes((T, 128))
    for m in range(M):
        bias = jnp.where(ctx_ref[m, 0] == 1, 0.0, -1e30).astype(f32)
        bcol = jnp.broadcast_to(bias, (128, T)).T
        for hd in range(HEADS):
            un = jnp.where((lane >= 3 * hd) & (lane < 3 * hd + 3), -1.0, 0.0)
            if m == 0:
                ku_s[hd] = un[:Q].astype(bf16)
            kb_s[hd] = jnp.where(lane == 12, bcol, un).astype(bf16)
        for b in range(4):
            col = bcol[b * Q : (b + 1) * Q, 0:1]
            diag_s[b] = jnp.where(subl((Q, Q)) == lanes((Q, Q)), 0.0, jnp.broadcast_to(col, (Q, Q)))
        for key in ("ext", "qkv", "dext", "do"):
            copies.wait((key, m))
        for base, nb, rows in neighbourhoods(seg_ref, m, T):
            every = pl.ds(base, nb * Q)
            out = pl.ds(pl.multiple_of(m * T + base, Q), nb * Q)
            w = nb * Q
            for hd in range(HEADS):
                cq = slice(hd * HD, (hd + 1) * HD)
                ck = slice(D + hd * HD, D + (hd + 1) * HD)
                cv = slice(2 * D + hd * HD, 2 * D + (hd + 1) * HD)
                for qb in range(nb):
                    here = pl.ds(rows[qb], Q)
                    qa = jnp.concatenate([qkv_ref[m, here, cq], ext_ref[m, here, :]], axis=1)
                    da = jnp.concatenate([do_ref[m, here, cq], dext_ref[m, here, :]], axis=1)
                    for kb in range(nb):
                        k = qkv_ref[m, pl.ds(rows[kb], Q), ck]
                        v = qkv_ref[m, pl.ds(rows[kb], Q), cv]
                        if kb == qb:
                            s = nt(jnp.concatenate([k, ku_s[hd]], axis=1), qa) + diag_s[rows[kb] // Q]
                        else:
                            s = nt(jnp.concatenate([k, kb_s[hd, pl.ds(rows[kb], Q), :]], axis=1), qa)
                        p = jnp.exp2(s)
                        dp = nt(jnp.concatenate([v, ku_s[hd]], axis=1), da)
                        p_s[hd % 2, kb * Q : (kb + 1) * Q, qb * Q : (qb + 1) * Q] = p.astype(bf16)
                        ds_s[hd % 2, kb * Q : (kb + 1) * Q, qb * Q : (qb + 1) * Q] = (p * dp).astype(bf16)
                p, ds = p_s[hd % 2, 0:w, 0:w], ds_s[hd % 2, 0:w, 0:w]
                dqkv_s[out, cv] = nn(p, do_ref[m, every, cq]).astype(bf16)
                dqkv_s[out, ck] = (nn(ds, qkv_ref[m, every, cq]) * LN2).astype(bf16)
                dqkv_s[out, cq] = (tn(qkv_ref[m, every, ck], ds) * scale).T.astype(bf16)
    for key in ("wa", "x", "da"):
        copies.wait(key)
    wev = wa_ref[:, 3 * D :].astype(f32).T.astype(bf16)[0:nf, :]
    dh_s[...] = (da_ref[...].astype(f32) + nt(dqkv_s[...], wa_ref[:, 0 : 3 * D])).astype(bf16)
    e = None
    for m in range(M):
        for j in range(nz):
            for s in range(2):
                r = (idx_ref[ZED] ^ j) * 2 + s
                dh = dh_s[pl.ds(pl.multiple_of(m * T + r * n, n), n), :]
                outs[j][s, m] = nt(wev, dh).astype(bf16)
                t = nn(x_ref[r, m], dh)
                e = t if e is None else e + t
    rest = jnp.concatenate([e[100:101], gv_ref[1:6, :], jnp.zeros((128 - nf - 6, D), f32)], axis=0)
    accx_s[...] = jnp.concatenate([e, rest], axis=0).T
    core = idx_ref[CORE]
    split_rows(accx_s, core, keep_ref, send_ref, slice(3 * D, 3 * D + 128))
    copies.wait("h")
    acc_s[...] = tn(h_ref[...].reshape(M * T, D), dqkv_s[...])
    split_rows(acc_s, core, keep_ref, send_ref, slice(0, 3 * D))


def core_kernel(keep_ref, got_ref, out_ref):
    nfeat, _, q, _ = out_ref.shape
    for g in range(nfeat):
        rows = slice(g * q, (g + 1) * q)
        out_ref[g] = (keep_ref[:, rows, :].astype(f32) + got_ref[:, rows, :].astype(f32)).astype(bf16)


def feat_kernel(na, idx_ref, a_ref, *refs):
    bs, outs = refs[:na], refs[na:]
    A = a_ref.shape[3]
    for j, out in enumerate(outs):
        out[:, 0:A] = sum(a_ref[g, idx_ref[ZED] ^ j].astype(f32) for g in range(a_ref.shape[0])).astype(bf16)
        if bs:
            out[:, A:] = bs[j][...]


def cut_kernel(idx_ref, x_ref, *outs):
    q = outs[0].shape[0]
    for g in range(len(outs)):
        for k, out in enumerate(outs):

            @pl.when((idx_ref[FEAT] ^ k) == g)
            def _():
                out[...] = x_ref[g * q : (g + 1) * q, :]


def feat_b_kernel(idx_ref, *refs):
    keep_ref, send_ref = refs[-2:]
    for z in range(keep_ref.shape[0]):
        for c, out in ((idx_ref[CORE], keep_ref), (1 - idx_ref[CORE], send_ref)):
            out[z] = sum(x[2 * z + c].astype(f32) for x in refs[:-2]).astype(bf16)


def core_b_kernel(idx_ref, keep_ref, got_ref, *outs):
    for j, out in enumerate(outs):
        z = idx_ref[ZED] ^ j
        out[...] = (keep_ref[z].astype(f32) + got_ref[z].astype(f32)).astype(bf16)


def rows_kernel(na, *refs):
    out = refs[-1]
    W = refs[0].shape[1]
    out[:, 0:W] = sum(x[...].astype(f32) for x in refs[:na]).astype(bf16)
    if len(refs) > na + 1:
        out[:, W:] = sum(x[...].astype(f32) for x in refs[na:-1]).astype(bf16)


def update(w, g, m, v, rate):
    m = 0.9 * m + 0.1 * g
    v = 0.95 * v + 0.05 * g * g
    return w - rate * ((m / (1.0 - 0.9**STEP)) / (jnp.sqrt(v / (1.0 - 0.95**STEP)) + 1e-8) + 0.1 * w), m, v


def adam_kernel(nfeat, idx_ref, *refs):
    gs, refs = refs[:nfeat], refs[nfeat:]
    ins, outs, held, g_s, sems = refs[:12], refs[12:24], refs[24:36], refs[36], refs[37]
    copies = Copies(sems)
    small = (0, 1, 2, 9, 10, 11)
    for i in small:
        copies.start(("in", i), ins[i], held[i])
    q = gs[0].shape[0]
    for k in range(nfeat):
        for f in range(nfeat):

            @pl.when((idx_ref[FEAT] ^ k) == f)
            def _():
                g_s[f * q : (f + 1) * q, :] = gs[k][...].astype(f32)

    D = ins[3].shape[1] // 4
    F, A = ins[0].shape[1], 3 * D + 128

    def step(i, g, rate):
        state = [(held if i + j in small else ins)[i + j][...] for j in range(3)]
        for j, x in enumerate(update(state[0], g, state[1], state[2], rate)):
            held[i + j][...] = x
            copies.start(("out", i + j), held[i + j], outs[i + j])

    step(6, g_s[:, A + D :], 0.02)
    step(3, jnp.concatenate([g_s[:, 0 : 3 * D], g_s[:, A : A + D]], axis=1), 0.25)
    for i in small:
        copies.wait(("in", i))
    x = g_s[:, 3 * D : A]
    step(0, x[:, 0:F], 0.08)
    step(9, x.T[104:110, :], 0.2)
    copies.wait_all()


def peer(x, axis, size, k):
    return lax.ppermute(x, axis, [(i, i ^ k) for i in range(size)])


def tie(x, *others):
    return lax.optimization_barrier((x, *others))[0]


def body(features, feat_mask, send_order, segment, context, cotangent, w_enc, w_attn, w_ffn, vectors, m_enc, v_enc, m_attn, v_attn, m_ffn, v_ffn, m_vec, v_vec):
    nfeat, nr = lax.axis_size("feat"), lax.axis_size("rows")
    nz = nr // 2
    fi, ri = lax.axis_index("feat"), lax.axis_index("rows")
    ci, zi = ri % 2, ri // 2
    idx = jnp.stack([ci, fi, zi]).astype(jnp.int32)
    M, tok, fl = features.shape
    T, F = tok // nfeat, fl * nfeat
    nf = -(-(F + 3) // 8) * 8
    Dl = w_attn.shape[0]
    D = Dl * nr
    n, q = T // nr, Dl // nfeat
    WA, WB = 3 * D + 128, 5 * D
    over_feat = lambda x: [x] + [peer(x, "feat", nfeat, k) for k in range(1, nfeat)]
    groups = [[2 * z + c for z in range(nz)] for c in range(2)]
    over_z = lambda x: [x] + [peer(x, "rows", nr, 2 * k) for k in range(1, nz)]
    to_z = lambda xs: [xs[0]] + [peer(xs[k], "rows", nr, 2 * k) for k in range(1, nz)]
    to_feat = lambda xs: [xs[0]] + [peer(xs[k], "feat", nfeat, k) for k in range(1, nfeat)]
    swap_z = lambda x: lax.all_to_all(x, "rows", 0, 0, axis_index_groups=groups, tiled=True)
    swap_feat = lambda x: lax.all_to_all(x, "feat", 0, 0, tiled=True)
    over_core = lambda x: peer(x, "rows", nr, 1)

    by_quarters = q % 16 == 0
    part_rows = q if by_quarters else Dl
    pack = call(
        functools.partial(pack_kernel, WA), shape((part_rows, WA + WB), bf16), idx, *[keep_far(a) for a in (w_attn, w_ffn, w_enc.T, vectors)],
        name="pack", flops=3 * 10**9, specs=[SMEM] + [HBM] * 4,
        scratch=[pltpu.VMEM(a, f32) for a in ((part_rows, 4 * D), (part_rows, 4 * D), w_enc.T.shape, vectors.shape)] + [pltpu.VMEM((Dl, 128), f32), pltpu.SemaphoreType.DMA((4,))],
    )
    order = send_order.reshape(M, nz, 2, n)
    order_mine = jnp.where(ci == 0, order[:, :, 0], order[:, :, 1]).reshape(M, 1, T // 2)
    order_other = jnp.where(ci == 0, order[:, :, 1], order[:, :, 0]).reshape(M, 1, T // 2)
    order_theirs = over_core(order_other)
    mask = feat_mask.transpose(2, 0, 1)
    xm = tie(features, pack).transpose(2, 0, 1) * mask.astype(bf16)
    xm = xm.reshape(fl, M, nfeat, T).transpose(2, 1, 0, 3)

    xm = swap_feat(xm)
    if by_quarters:
        pa, pb = call(join_kernel, [shape((nz, q, WA), bf16), shape((nz, q, WB), bf16)], idx, *over_z(pack), smem=1, name="join", flops=10**9)
        xm = tie(xm, pa)
        pa = over_feat(pa)
    x = call(
        sort_kernel, shape((nz, 2, M, nf, n), bf16), idx, order_mine, order_theirs, xm, over_core(xm),
        smem=1, scratch=[pltpu.VMEM((nf, T), f32)], name="sort", flops=3 * 10**9,
    )
    if by_quarters:
        pa = [pa[0]] + [tie(a, x) for a in pa[1:]]
        pa = pa + [over_core(a) for a in pa]
        pb = over_feat(tie(pb, x))
    else:
        pa = [lax.all_gather(pack[:, :WA], "rows", axis=0, tiled=True)]
        pb = [lax.all_gather(pack[:, WA:], "rows", axis=0, tiled=True)]
    x = swap_z(x).reshape(nr, M, nf, n)

    Q = T // 4
    dma = lambda k: pltpu.SemaphoreType.DMA((k,))
    ram = lambda d, *r: pltpu.VMEM(r, d)
    vec, h, o, qkv, ext, wa, x = call(
        attend_kernel,
        [far((8, D), f32), far((M, T, D), bf16), far((M, T, D), bf16), far((M, T, 3 * D), bf16), far((M, T, 128), bf16), far((D, WA), bf16), far((nr, M, nf, n), bf16)],
        idx, segment, context, x, *pa,
        smem=2, name="attend", flops=16 * 10**9, mib=36, outs=[VMEM] + [HBM] * 6,
        scratch=[ram(bf16, M, T, D), ram(bf16, M, T, D), ram(bf16, M, T, 3 * D), ram(bf16, M, T, 128), ram(bf16, D, WA), ram(bf16, 128, D), ram(bf16, T, 128), ram(f32, 4, Q, Q), ram(bf16, 2, BIG * Q, BIG * Q), dma(3 + 3 * M)],
    )

    if by_quarters:
        pb = [pb[0]] + [tie(a, o) for a in pb[1:]]
        pb = pb + [over_core(a) for a in pb]
    ng = nfeat if by_quarters else 1
    *grads_b, act, da, do, dext, gv = call(
        functools.partial(feed_kernel, len(pb), ng),
        [far((nr, q, WB) if by_quarters else (D, WB), bf16)] * ng
        + [far((M, 1, T, D), f32), far((M * T, D), bf16), far((M, T, D), bf16), far((M, T, 128), bf16), far((8, D), f32)],
        idx, keep_far(vec), *[keep_far(a) for a in (h, o, cotangent)], *pb,
        name="feed", flops=29 * 10**9, mib=56, specs=[SMEM, VMEM] + [HBM] * 3 + [VMEM] * len(pb), outs=[HBM] * (ng + 4) + [VMEM],
        scratch=[ram(bf16, M, T, D), ram(bf16, M, T, D), ram(bf16, M * T, D), ram(bf16, M, T, D), ram(bf16, M, T, 128), ram(bf16, *((nr, nfeat, q, WB) if by_quarters else (D, WB))), ram(bf16, D, WB), ram(bf16, M, 1, T, D), ram(bf16, M * T, D), ram(bf16, M * T, 2 * D), ram(bf16, M * T, D), ram(bf16, M * T, 2 * D), ram(f32, 2, T // 2, D), dma(3 * ng + 11 * M)],
    )
    if by_quarters:
        grads_b = to_feat(grads_b)
    else:
        sum_b = lax.psum_scatter(grads_b[0], "rows", scatter_dimension=0, tiled=True)

    *dxs, keep_a, send_a = call(
        functools.partial(back_kernel, nz),
        [shape((2, M, nf, n), bf16)] * nz + [shape((nz, Dl, WA), bf16)] * 2,
        idx, segment, context, keep_far(gv), *[keep_far(a) for a in (do, dext, da, qkv, ext, h, wa, x)],
        name="back", flops=29 * 10**9, mib=50, specs=[SMEM] * 2 + [VMEM] * 2 + [HBM] * 8,
        scratch=[ram(bf16, M, T, D), ram(bf16, M, T, 128), ram(bf16, M * T, D), ram(bf16, M, T, 3 * D), ram(bf16, M, T, 128), ram(bf16, M, T, D), ram(bf16, D, WA), ram(bf16, nr, M, nf, n), ram(bf16, M * T, 3 * D),
            ram(bf16, HEADS, T, 128), ram(bf16, HEADS, Q, 128), ram(f32, 4, Q, Q), ram(bf16, 2, BIG * Q, BIG * Q), ram(bf16, 2, BIG * Q, BIG * Q),
            ram(f32, D, 3 * D), ram(f32, D, 128), ram(bf16, M * T, D), dma(4 + 4 * M)],
    )

    got_a = over_core(send_a)
    if by_quarters:
        grads_b[0] = tie(grads_b[0], keep_a)
        keep_b, send_b = call(feat_b_kernel, [shape((nz, q, WB), bf16)] * 2, idx, *grads_b, smem=1, name="feat_sum_b", flops=10**9)
        got_b = over_core(send_b)
        keep_a = tie(keep_a, keep_b)
    part = call(core_kernel, shape((nfeat, nz, q, WA), bf16), keep_a, got_a, name="core_sum", flops=10**9)
    if by_quarters:
        sums = call(core_b_kernel, [shape((q, WB), bf16)] * nz, idx, tie(keep_b, part), got_b, smem=1, name="core_sum_b", flops=10**9)
        dxs[0] = tie(dxs[0], *sums)
    else:
        dxs[0] = tie(dxs[0], part)
        sums = to_feat(call(cut_kernel, [shape((q, WB), bf16)] * nfeat, idx, tie(sum_b, part), smem=1, name="cut", flops=10**9))
    dxs[1:] = [tie(a, part) for a in dxs[1:]]
    dxs = to_z(dxs)
    part = swap_feat(part)
    mine, other = call(pick_kernel, [shape((nz, M, nf, n), bf16)] * 2, idx, *dxs, smem=1, name="pick", flops=10**9)
    dx = call(
        unsort_kernel, shape((nfeat, M, fl, T), bf16), order_mine, order_other, mine, over_core(other),
        scratch=[pltpu.VMEM((nf, T), f32)], name="unsort", flops=3 * 10**9,
    )
    part = tie(part, dx)
    dx = swap_feat(dx)
    beside, sums = (sums, []) if by_quarters else ([], sums)
    part = to_z(call(functools.partial(feat_kernel, len(beside)), [shape((q, WA + len(beside) // nz * WB), bf16)] * nz, idx, part, *beside, smem=1, name="feat_sum", flops=10**9))
    grads = over_feat(call(functools.partial(rows_kernel, nz), shape((q, WA + WB), bf16), *part, *sums, name="rows_sum", flops=10**9))
    x_grad = dx.transpose(2, 1, 0, 3).reshape(fl, M, tok).astype(f32) * mask.astype(f32)
    state = [w_enc.T, m_enc.T, v_enc.T, w_attn, m_attn, v_attn, w_ffn, m_ffn, v_ffn, vectors, m_vec, v_vec]
    far_state = [keep_far(a) if a.size < Dl * D else a for a in state]
    new = call(
        functools.partial(adam_kernel, nfeat), [far(a.shape, f32) for a in state], idx, *grads, *far_state,
        specs=[SMEM] + [VMEM] * nfeat + [HBM if a.size < Dl * D else VMEM for a in state], outs=[HBM] * 12, scratch=[pltpu.VMEM(a.shape, f32) for a in state] + [pltpu.VMEM((Dl, WA + WB), f32), dma(18)], name="adamw", flops=4 * 10**9,
    )
    return (act, x_grad.transpose(1, 2, 0), *[x.T for x in new[:3]], *new[3:])


def solution(mesh):
    tok, grp = P(None, "rows", "feat"), P(None, "feat", "rows", None)
    col, row = P(None, "rows"), P("rows", None)
    return jax.shard_map(
        body,
        mesh=mesh,
        in_specs=(tok, tok, P(None, "rows", "feat", None), grp, grp, grp, col, row, row, col, col, col, row, row, row, row, col, col),
        out_specs=(grp, tok) + (col,) * 3 + (row,) * 6 + (col,) * 3,
        check_vma=False,
    )
```

```python
import functools
import math

import jax
import jax.numpy as jnp
from jax import lax
from jax.experimental import pallas as pl
from jax.experimental.pallas import tpu as pltpu
from jax.sharding import PartitionSpec as P

bf16 = jnp.bfloat16
f32 = jnp.float32
HEADS = 4
STEP = 10
BIG = 3
LN2 = math.log(2.0)
LOG2E = math.log2(math.e)
SMEM = pl.BlockSpec(memory_space=pltpu.SMEM)
VMEM = pl.BlockSpec(memory_space=pltpu.VMEM)
HBM = pl.BlockSpec(memory_space=pltpu.HBM)


def dot(a, b, ca, cb):
    return lax.dot_general(a, b, (((ca,), (cb,)), ((), ())), preferred_element_type=f32)


def nn(a, b):
    return dot(a, b, 1, 0)


def nt(a, b):
    return dot(a, b, 1, 1)


def tn(a, b):
    return dot(a, b, 0, 0)


def lanes(shape):
    return lax.broadcasted_iota(jnp.int32, shape, 1)


def subl(shape):
    return lax.broadcasted_iota(jnp.int32, shape, 0)


def split3(x):
    a = x.astype(bf16).astype(f32)
    r = x - a
    b = r.astype(bf16).astype(f32)
    return a, b, r - b


def call(kernel, out_shape, *args, smem=0, scratch=(), name=None, flops=10**6, moved=10**6, mib=16, specs=None, outs=None):
    single = not isinstance(out_shape, (list, tuple))
    return pl.pallas_call(
        kernel,
        out_shape=out_shape,
        in_specs=specs or [SMEM] * smem + [VMEM] * (len(args) - smem),
        out_specs=outs or (VMEM if single else [VMEM] * len(out_shape)),
        scratch_shapes=list(scratch),
        compiler_params=pltpu.CompilerParams(vmem_limit_bytes=mib << 20),
        cost_estimate=pl.CostEstimate(flops=flops, bytes_accessed=moved, transcendentals=0),
        name=name,
    )(*args)


def shape(s, d):
    return jax.ShapeDtypeStruct(tuple(s), d)


def far(s, d):
    return pltpu.HBM(tuple(s), d)


def keep_far(x):
    return pltpu.with_memory_space_constraint(x, pltpu.HBM)


class Copies:
    def __init__(self, sems):
        self.sems, self.used, self.open = sems, 0, {}

    def start(self, key, src, dst):
        self.open[key] = pltpu.make_async_copy(src, dst, self.sems.at[self.used])
        self.used += 1
        self.open[key].start()

    def wait(self, key):
        if key in self.open:
            self.open.pop(key).wait()

    def wait_all(self):
        for key in list(self.open):
            self.wait(key)


CORE, FEAT, ZED = 0, 1, 2


def starts(seg_ref, m, T):
    q = T // 4
    first = seg_ref[m, 0, 0, 0] == seg_ref[m, 0, 0, q]
    big = jnp.where(first, 0, q)
    small = jnp.where(first, 3 * q, 0)
    return pl.multiple_of(big, q), pl.multiple_of(small, q)


def neighbourhoods(seg_ref, m, T):
    q = T // 4
    big, small = starts(seg_ref, m, T)
    for base, nb in ((big, BIG), (small, 4 - BIG)):
        yield base, nb, [pl.multiple_of(base + b * q, q) for b in range(nb)]


def split_rows(acc, core, keep_ref, send_ref, cols):
    nz, dl = keep_ref.shape[0], keep_ref.shape[1]
    for z in range(nz):
        mine = pl.multiple_of((2 * z + core) * dl, 8)
        other = pl.multiple_of((2 * z + 1 - core) * dl, 8)
        keep_ref[z, :, cols] = acc[pl.ds(mine, dl), :].astype(bf16)
        send_ref[z, :, cols] = acc[pl.ds(other, dl), :].astype(bf16)


def pack_kernel(WA, idx_ref, attn_ref, ffn_ref, enc_ref, vec_ref, out_ref, attn_s, ffn_s, enc_s, vec_s, x_s, sems):
    D3, Dl, q = WA - 128, enc_s.shape[0], out_ref.shape[0]
    D = D3 // 3
    rows = slice(None) if q == Dl else pl.ds(pl.multiple_of(idx_ref[FEAT] * q, q), q)
    copies = Copies(sems)
    for key, src, dst in (("e", enc_ref, enc_s), ("v", vec_ref, vec_s), ("a", attn_ref.at[rows, :], attn_s), ("f", ffn_ref.at[rows, :], ffn_s)):
        copies.start(key, src, dst)
    copies.wait("e")
    copies.wait("v")
    p = split3(vec_s[...])
    none = jnp.zeros((1, Dl), f32)
    t = jnp.concatenate([x[0:1] for x in p] + [none] + [x[1:6] for x in p] + [jnp.zeros((9, Dl), f32)], axis=0)
    x_s[...] = jnp.concatenate([enc_s[...], t.T], axis=1)
    out_ref[:, D3:WA] = x_s[rows, :].astype(bf16)
    copies.wait("a")
    out_ref[:, 0:D3] = attn_s[:, 0:D3].astype(bf16)
    out_ref[:, WA : WA + D] = attn_s[:, D3:].astype(bf16)
    copies.wait("f")
    out_ref[:, WA + D :] = ffn_s[...].astype(bf16)


def join_kernel(idx_ref, *refs):
    a_ref, b_ref = refs[-2:]
    A = a_ref.shape[3]
    for j, ref in enumerate(refs[:-2]):
        z = idx_ref[ZED] ^ j
        b_ref[z] = ref[:, A:]
        for g in range(a_ref.shape[0]):
            a_ref[g, z] = ref[:, 0:A]


def assemble(idx_ref, pieces, dst):
    if len(pieces) == 1:
        dst[...] = pieces[0][...]
        return
    if len(pieces) == 2:
        nfeat, nz, q, _ = pieces[0].shape
        for c in range(2):
            for g in range(nfeat):
                for j in range(nz):
                    r = (j * 2 + (idx_ref[CORE] ^ c)) * (nfeat * q) + g * q
                    dst[pl.ds(pl.multiple_of(r, q), q), :] = pieces[c][g, j]
        return
    nz, q, _ = pieces[0].shape
    nfeat = len(pieces) // 2
    for c in range(2):
        for k in range(nfeat):
            for j in range(nz):
                r = (j * 2 + (idx_ref[CORE] ^ c)) * (nfeat * q) + (idx_ref[FEAT] ^ k) * q
                dst[pl.ds(pl.multiple_of(r, q), q), :] = pieces[c * nfeat + k][j]


def one_hot(order, T):
    return jnp.where(subl((T, order.shape[1])) == order, 1.0, 0.0).astype(bf16)


def sort_kernel(nfeat, idx_ref, mine_ref, theirs_ref, *refs):
    xs, outs, s_ref, y_ref = refs[: 2 * nfeat], refs[2 * nfeat : -2], refs[-2], refs[-1]
    M, f, T = xs[0].shape
    nz, nf, n = y_ref.shape
    s_ref[nfeat * f :, :] = jnp.where(subl((nf - nfeat * f, T)) < 3, 1.0, 0.0)
    for s, order_ref in enumerate((mine_ref, theirs_ref)):
        core = idx_ref[CORE] ^ s
        for m in range(M):
            for k in range(nfeat):
                for g in range(nfeat):

                    @pl.when((idx_ref[FEAT] ^ k) == g)
                    def _():
                        s_ref[g * f : (g + 1) * f, :] = xs[s * nfeat + k][m].astype(f32)

            y = nn(s_ref[...].astype(bf16), one_hot(order_ref[m], T)).astype(bf16)
            for z in range(nz):
                y_ref[z] = y[:, z * n : (z + 1) * n]
            for j, out in enumerate(outs):
                out[core, m] = y_ref[idx_ref[ZED] ^ j]


def pick_kernel(idx_ref, *refs):
    mine_ref, other_ref = refs[-2:]
    for j, ref in enumerate(refs[:-2]):
        mine_ref[idx_ref[ZED] ^ j] = ref[idx_ref[CORE]]
        other_ref[idx_ref[ZED] ^ j] = ref[1 - idx_ref[CORE]]


def unsort_kernel(mine_ref, other_ref, x_ref, got_ref, out_ref, s_ref):
    nz = x_ref.shape[0]
    nfeat, M, f, T = out_ref.shape
    for m in range(M):
        mine = jnp.concatenate([x_ref[z, m] for z in range(nz)], axis=1)
        other = jnp.concatenate([got_ref[z, m] for z in range(nz)], axis=1)
        s_ref[...] = nt(mine, one_hot(mine_ref[m], T)) + nt(other, one_hot(other_ref[m], T))
        for g in range(nfeat):
            out_ref[g, m] = s_ref[g * f : (g + 1) * f, :].astype(bf16)


def attend_kernel(nz, idx_ref, seg_ref, ctx_ref, *refs):
    ys, refs = refs[:nz], refs[nz:]
    pieces, refs = refs[:-17], refs[-17:]
    vec_ref, h_out, o_out, qkv_out, ext_out, wa_out, x_out, h_ref, o_ref, qkv_ref, ext_ref, wa_ref, wev_ref, kext_s, diag_s, e_s, sems = refs
    M, T, D = h_ref.shape
    Q, HD = T // 4, D // HEADS
    nf, n = ys[0].shape[2], ys[0].shape[3]
    copies = Copies(sems)
    for j in range(nz):
        copies.start(("x", j), ys[j], x_out.at[pl.ds(2 * (idx_ref[ZED] ^ j), 2)])
    assemble(idx_ref, pieces, wa_ref)
    copies.start("wa", wa_ref, wa_out)
    t = wa_ref[:, 3 * D :].astype(f32).T
    wev_ref[...] = t.astype(bf16)
    vec_ref[...] = jnp.concatenate([jnp.zeros((1, D), f32), t[104:109] + t[109:114] + t[114:119], jnp.zeros((2, D), f32)], axis=0)
    wev = wev_ref[0:nf, :]
    c = LOG2E * HD**-0.5
    qext = jnp.where(lanes((Q, 128)) == 0, 1.0, 0.0).astype(bf16)
    lane = lanes((Q, 128))
    for m in range(M):
        for j in range(nz):
            for s in range(2):
                r = pl.multiple_of(((idx_ref[ZED] ^ j) * 2 + s) * n, n)
                h_ref[m, pl.ds(r, n), :] = tn(ys[j][s, m], wev).astype(bf16)
    copies.start("h", h_ref, h_out)
    for m in range(M):
        h = h_ref[m]
        qkv_ref[m, :, 0:D] = (nn(h, wa_ref[:, 0:D]) * c).astype(bf16)
        qkv_ref[m, :, D : 3 * D] = nn(h, wa_ref[:, D : 3 * D]).astype(bf16)
        copies.start(("qkv", m), qkv_ref.at[m], qkv_out.at[m])
        bias = jnp.where(ctx_ref[m, 0] == 1, 0.0, -1e30).astype(f32)
        bcol = jnp.broadcast_to(bias, (128, T)).T
        kext_s[...] = jnp.where(lanes((T, 128)) == 0, bcol, 0.0).astype(bf16)
        for b in range(4):
            row = jnp.broadcast_to(bias[:, b * Q : (b + 1) * Q], (Q, Q))
            diag_s[b] = jnp.where(subl((Q, Q)) == lanes((Q, Q)), 0.0, row)
        for base, nb, rows in neighbourhoods(seg_ref, m, T):
            every = pl.ds(base, nb * Q)
            exts = [jnp.where(lane == 12, 1.0, 0.0) for _ in range(nb)]
            for hd in range(HEADS):
                cq = slice(hd * HD, (hd + 1) * HD)
                ck = slice(D + hd * HD, D + (hd + 1) * HD)
                cv = slice(2 * D + hd * HD, 2 * D + (hd + 1) * HD)
                tops = []
                for qb in range(nb):
                    q = qkv_ref[m, pl.ds(rows[qb], Q), cq]
                    qa = jnp.concatenate([q, qext], axis=1)
                    s = []
                    for kb in range(nb):
                        k = qkv_ref[m, pl.ds(rows[kb], Q), ck]
                        if kb == qb:
                            s.append(nt(q, k) + diag_s[rows[kb] // Q])
                        else:
                            s.append(nt(qa, jnp.concatenate([k, kext_s[pl.ds(rows[kb], Q), :]], axis=1)))
                    top = jnp.max(functools.reduce(jnp.maximum, s), axis=1, keepdims=True)
                    tops.append(top)
                    for kb in range(nb):
                        e_s[hd % 2, qb * Q : (qb + 1) * Q, kb * Q : (kb + 1) * Q] = jnp.exp2(s[kb] - top).astype(bf16)
                v = qkv_ref[m, every, cv]
                acc = nn(e_s[hd % 2, 0 : nb * Q, 0 : nb * Q], jnp.concatenate([v, jnp.ones((nb * Q, 128), bf16)], axis=1))
                total = acc[:, HD:]
                o_ref[m, every, cq] = (acc[:, :HD] / total).astype(bf16)
                for qb in range(nb):
                    lse = tops[qb] + jnp.log2(total[qb * Q : (qb + 1) * Q])
                    for j, part in enumerate(split3(lse)):
                        exts[qb] = jnp.where(lane == 3 * hd + j, part, exts[qb])
            for qb in range(nb):
                ext_ref[m, pl.ds(rows[qb], Q), :] = exts[qb].astype(bf16)
        copies.start(("ext", m), ext_ref.at[m], ext_out.at[m])
        copies.start(("o", m), o_ref.at[m], o_out.at[m])
    copies.wait_all()


def gelu_parts(u):
    cdf = 0.5 + 0.5 * lax.erf(u * (2.0**-0.5))
    pdf = jnp.exp2(u * u * (-0.5 * LOG2E)) * (1.0 / math.sqrt(2.0 * math.pi))
    return cdf, pdf


def colsum(x):
    return jnp.sum(x.reshape(x.shape[0] // 8, 8, x.shape[1]), axis=0)


def mean(x):
    return jnp.mean(x, axis=1, keepdims=True)


def feed_kernel(np_, ng, idx_ref, vec_ref, h_hbm, o_hbm, cot_hbm, *refs):
    pieces, refs = refs[:np_], refs[np_:]
    gb_outs, refs = refs[:ng], refs[ng:]
    act_ref, da_out, do_out, dext_out, gv_ref, h_ref, o_ref, da_ref, do_ref, dext_ref, gb_ref, wb_s, cot_ref, y1_s, gr_s, db_s, du_s, act_s, sems = refs
    M, T, D = h_ref.shape
    F, HD, B = 2 * D, D // HEADS, T // 2
    wo, w1, w2 = slice(0, D), slice(D, D + F), slice(D + F, D + 2 * F)
    copies = Copies(sems)
    for m in range(M):
        copies.start(("o", m), o_hbm.at[m], o_ref.at[m])
        copies.start(("h", m), h_hbm.at[m], h_ref.at[m])
        copies.start(("cot", m), cot_hbm.at[m], cot_ref.at[m])
    assemble(idx_ref, pieces, wb_s)
    g1, s1, g2, s2, b2 = (vec_ref[j : j + 1, :] for j in range(1, 6))
    lane = lanes((B, 128))
    vsum = [0.0] * 5

    def chain(m, b):
        r = slice(b * B, (b + 1) * B)
        w = slice(m * T + b * B, m * T + (b + 1) * B)
        copies.wait(("o", m))
        o = o_ref[m, r, :]
        t = nn(o, wb_s[:, wo])
        yield
        copies.wait(("h", m))
        a = h_ref[m, r, :].astype(f32) + t
        ac = a - mean(a)
        i1 = lax.rsqrt(mean(ac * ac) + 1e-5)
        xh1 = ac * i1
        y1 = xh1 * g1 + s1
        y1b = y1.astype(bf16)
        y1_s[w, :] = y1b
        u = nn(y1b, wb_s[:, w1])
        yield
        cdf, pdf = gelu_parts(u)
        gr = (u * cdf).astype(bf16)
        gr_s[w, :] = gr
        dgelu = cdf + u * pdf
        t = nt(gr, wb_s[:, w2])
        yield
        z = y1 + t + b2
        zc = z - mean(z)
        i2 = lax.rsqrt(mean(zc * zc) + 1e-5)
        xh2 = zc * i2
        copies.wait(("act", b))
        act_s[b] = xh2 * g2 + s2
        copies.start(("act", b), act_s.at[b], act_ref.at[m, 0, pl.ds(b * B, B), :])
        copies.wait(("cot", m))
        c = cot_ref[m, 0, r, :].astype(f32)
        vsum[2] += colsum(c * xh2)
        vsum[3] += colsum(c)
        cg = c * g2
        db = i2 * (cg - mean(cg) - xh2 * mean(cg * xh2))
        vsum[4] += colsum(db)
        dbr = db.astype(bf16)
        db_s[w, :] = dbr
        t = nn(dbr, wb_s[:, w2])
        yield
        du = (t * dgelu).astype(bf16)
        du_s[w, :] = du
        t = nt(du, wb_s[:, w1])
        yield
        dy = db + t
        vsum[0] += colsum(dy * xh1)
        vsum[1] += colsum(dy)
        cg = dy * g1
        da = i1 * (cg - mean(cg) - xh1 * mean(cg * xh1))
        dar = da.astype(bf16)
        da_ref[w, :] = dar
        do = nt(dar, wb_s[:, wo]).astype(bf16)
        yield
        do_ref[m, r, :] = do
        od = o.astype(f32) * do.astype(f32)
        ext = jnp.zeros((B, 128), f32)
        for hd in range(HEADS):
            delta = jnp.sum(od[:, hd * HD : (hd + 1) * HD], axis=1, keepdims=True)
            for j, part in enumerate(split3(delta)):
                ext = jnp.where(lane == 3 * hd + j, part, ext)
        dext_ref[m, r, :] = ext.astype(bf16)
        copies.start(("da", m, b), da_ref.at[w, :], da_out.at[w, :])
        copies.start(("do", m, b), do_ref.at[m, r, :], do_out.at[m, r, :])
        copies.start(("dext", m, b), dext_ref.at[m, r, :], dext_out.at[m, r, :])

    for m in range(M):
        gens = [chain(m, b) for b in range(2)]
        for _ in range(7):
            for g in gens:
                next(g, None)
    gv_ref[...] = jnp.concatenate([jnp.zeros((1, D), f32)] + [jnp.sum(x, axis=0, keepdims=True) for x in vsum] + [jnp.zeros((2, D), f32)], axis=0)
    left = {wo.start: (o_ref[...].reshape(M * T, D), da_ref), w1.start: (y1_s, du_s), w2.start: (db_s, gr_s)}
    for cols in (w2, w1, wo):
        a, b = left[cols.start]
        g = tn(a[...], b[...]).astype(bf16)
        if ng == 1:
            gb_ref[:, cols] = g
            copies.start(("gb", cols.start), gb_ref.at[:, cols], gb_outs[0].at[:, cols])
        else:
            nr, q, _ = gb_outs[0].shape
            gb_ref[:, :, :, cols] = g.reshape(nr, ng, q, g.shape[1])
            for k, out in enumerate(gb_outs):
                copies.start(("gb", cols.start, k), gb_ref.at[:, idx_ref[FEAT] ^ k, :, cols], out.at[:, :, cols])
    copies.wait_all()


def back_kernel(nz, idx_ref, seg_ref, ctx_ref, gv_ref, do_hbm, dext_hbm, da_hbm, qkv_hbm, ext_hbm, h_hbm, wa_hbm, x_hbm, *refs):
    outs, refs = refs[:nz], refs[nz:]
    keep_ref, send_ref, do_ref, dext_ref, da_ref, qkv_ref, ext_ref, h_ref, wa_ref, x_ref, dqkv_s, kb_s, ku_s, diag_s, p_s, ds_s, acc_s, accx_s, dh_s, sems = refs
    M, T, D = do_ref.shape
    Q, HD = T // 4, D // HEADS
    nf, n = x_ref.shape[2], x_ref.shape[3]
    scale = HD**-0.5
    copies = Copies(sems)
    for m in range(M):
        for key, src, dst in (("ext", ext_hbm, ext_ref), ("qkv", qkv_hbm, qkv_ref), ("dext", dext_hbm, dext_ref), ("do", do_hbm, do_ref)):
            copies.start((key, m), src.at[m], dst.at[m])
    for key, src, dst in (("da", da_hbm, da_ref), ("h", h_hbm, h_ref), ("wa", wa_hbm, wa_ref), ("x", x_hbm, x_ref)):
        copies.start(key, src, dst)
    lane = lanes((T, 128))
    for m in range(M):
        bias = jnp.where(ctx_ref[m, 0] == 1, 0.0, -1e30).astype(f32)
        bcol = jnp.broadcast_to(bias, (128, T)).T
        for hd in range(HEADS):
            un = jnp.where((lane >= 3 * hd) & (lane < 3 * hd + 3), -1.0, 0.0)
            if m == 0:
                ku_s[hd] = un[:Q].astype(bf16)
            kb_s[hd] = jnp.where(lane == 12, bcol, un).astype(bf16)
        for b in range(4):
            col = bcol[b * Q : (b + 1) * Q, 0:1]
            diag_s[b] = jnp.where(subl((Q, Q)) == lanes((Q, Q)), 0.0, jnp.broadcast_to(col, (Q, Q)))
        for key in ("ext", "qkv", "dext", "do"):
            copies.wait((key, m))
        for base, nb, rows in neighbourhoods(seg_ref, m, T):
            every = pl.ds(base, nb * Q)
            out = pl.ds(pl.multiple_of(m * T + base, Q), nb * Q)
            w = nb * Q
            for hd in range(HEADS):
                cq = slice(hd * HD, (hd + 1) * HD)
                ck = slice(D + hd * HD, D + (hd + 1) * HD)
                cv = slice(2 * D + hd * HD, 2 * D + (hd + 1) * HD)
                for qb in range(nb):
                    here = pl.ds(rows[qb], Q)
                    qa = jnp.concatenate([qkv_ref[m, here, cq], ext_ref[m, here, :]], axis=1)
                    da = jnp.concatenate([do_ref[m, here, cq], dext_ref[m, here, :]], axis=1)
                    for kb in range(nb):
                        k = qkv_ref[m, pl.ds(rows[kb], Q), ck]
                        v = qkv_ref[m, pl.ds(rows[kb], Q), cv]
                        if kb == qb:
                            s = nt(jnp.concatenate([k, ku_s[hd]], axis=1), qa) + diag_s[rows[kb] // Q]
                        else:
                            s = nt(jnp.concatenate([k, kb_s[hd, pl.ds(rows[kb], Q), :]], axis=1), qa)
                        p = jnp.exp2(s)
                        dp = nt(jnp.concatenate([v, ku_s[hd]], axis=1), da)
                        p_s[hd % 2, kb * Q : (kb + 1) * Q, qb * Q : (qb + 1) * Q] = p.astype(bf16)
                        ds_s[hd % 2, kb * Q : (kb + 1) * Q, qb * Q : (qb + 1) * Q] = (p * dp).astype(bf16)
                p, ds = p_s[hd % 2, 0:w, 0:w], ds_s[hd % 2, 0:w, 0:w]
                dqkv_s[out, cv] = nn(p, do_ref[m, every, cq]).astype(bf16)
                dqkv_s[out, ck] = (nn(ds, qkv_ref[m, every, cq]) * LN2).astype(bf16)
                dqkv_s[out, cq] = (tn(qkv_ref[m, every, ck], ds) * scale).T.astype(bf16)
    for key in ("wa", "x", "da"):
        copies.wait(key)
    wev = wa_ref[:, 3 * D :].astype(f32).T.astype(bf16)[0:nf, :]
    dh_s[...] = (da_ref[...].astype(f32) + nt(dqkv_s[...], wa_ref[:, 0 : 3 * D])).astype(bf16)
    e = None
    for m in range(M):
        for j in range(nz):
            for s in range(2):
                r = (idx_ref[ZED] ^ j) * 2 + s
                dh = dh_s[pl.ds(pl.multiple_of(m * T + r * n, n), n), :]
                outs[j][s, m] = nt(wev, dh).astype(bf16)
                t = nn(x_ref[r, m], dh)
                e = t if e is None else e + t
    rest = jnp.concatenate([e[100:101], gv_ref[1:6, :], jnp.zeros((128 - nf - 6, D), f32)], axis=0)
    accx_s[...] = jnp.concatenate([e, rest], axis=0).T
    core = idx_ref[CORE]
    split_rows(accx_s, core, keep_ref, send_ref, slice(3 * D, 3 * D + 128))
    copies.wait("h")
    acc_s[...] = tn(h_ref[...].reshape(M * T, D), dqkv_s[...])
    split_rows(acc_s, core, keep_ref, send_ref, slice(0, 3 * D))


def core_kernel(keep_ref, got_ref, out_ref):
    nfeat, _, q, _ = out_ref.shape
    for g in range(nfeat):
        rows = slice(g * q, (g + 1) * q)
        out_ref[g] = (keep_ref[:, rows, :].astype(f32) + got_ref[:, rows, :].astype(f32)).astype(bf16)


def feat_kernel(na, idx_ref, a_ref, *refs):
    bs, outs = refs[:na], refs[na:]
    A = a_ref.shape[3]
    for j, out in enumerate(outs):
        out[:, 0:A] = sum(a_ref[g, idx_ref[ZED] ^ j].astype(f32) for g in range(a_ref.shape[0])).astype(bf16)
        if bs:
            out[:, A:] = bs[j][...]


def cut_kernel(idx_ref, x_ref, *outs):
    q = outs[0].shape[0]
    for g in range(len(outs)):
        for k, out in enumerate(outs):

            @pl.when((idx_ref[FEAT] ^ k) == g)
            def _():
                out[...] = x_ref[g * q : (g + 1) * q, :]


def feat_b_kernel(idx_ref, *refs):
    keep_ref, send_ref = refs[-2:]
    for z in range(keep_ref.shape[0]):
        for c, out in ((idx_ref[CORE], keep_ref), (1 - idx_ref[CORE], send_ref)):
            out[z] = sum(x[2 * z + c].astype(f32) for x in refs[:-2]).astype(bf16)


def core_b_kernel(idx_ref, keep_ref, got_ref, *outs):
    for j, out in enumerate(outs):
        z = idx_ref[ZED] ^ j
        out[...] = (keep_ref[z].astype(f32) + got_ref[z].astype(f32)).astype(bf16)


def rows_kernel(na, *refs):
    out = refs[-1]
    W = refs[0].shape[1]
    out[:, 0:W] = sum(x[...].astype(f32) for x in refs[:na]).astype(bf16)
    if len(refs) > na + 1:
        out[:, W:] = sum(x[...].astype(f32) for x in refs[na:-1]).astype(bf16)


def update(w, g, m, v, rate):
    m = 0.9 * m + 0.1 * g
    v = 0.95 * v + 0.05 * g * g
    return w - rate * ((m / (1.0 - 0.9**STEP)) / (jnp.sqrt(v / (1.0 - 0.95**STEP)) + 1e-8) + 0.1 * w), m, v


def adam_kernel(nfeat, idx_ref, *refs):
    gs, refs = refs[:nfeat], refs[nfeat:]
    ins, outs, held, g_s, sems = refs[:12], refs[12:24], refs[24:36], refs[36], refs[37]
    copies = Copies(sems)
    small = (0, 1, 2, 9, 10, 11)
    for i in small:
        copies.start(("in", i), ins[i], held[i])
    q = gs[0].shape[0]
    for k in range(nfeat):
        for f in range(nfeat):

            @pl.when((idx_ref[FEAT] ^ k) == f)
            def _():
                g_s[f * q : (f + 1) * q, :] = gs[k][...].astype(f32)

    D = ins[3].shape[1] // 4
    F, A = ins[0].shape[1], 3 * D + 128

    def step(i, g, rate):
        state = [(held if i + j in small else ins)[i + j][...] for j in range(3)]
        for j, x in enumerate(update(state[0], g, state[1], state[2], rate)):
            held[i + j][...] = x
            copies.start(("out", i + j), held[i + j], outs[i + j])

    step(6, g_s[:, A + D :], 0.02)
    step(3, jnp.concatenate([g_s[:, 0 : 3 * D], g_s[:, A : A + D]], axis=1), 0.25)
    for i in small:
        copies.wait(("in", i))
    x = g_s[:, 3 * D : A]
    step(0, x[:, 0:F], 0.08)
    step(9, x.T[104:110, :], 0.2)
    copies.wait_all()


def peer(x, axis, size, k):
    return lax.ppermute(x, axis, [(i, i ^ k) for i in range(size)])


def tie(x, *others):
    return lax.optimization_barrier((x, *others))[0]


def body(features, feat_mask, send_order, segment, context, cotangent, w_enc, w_attn, w_ffn, vectors, m_enc, v_enc, m_attn, v_attn, m_ffn, v_ffn, m_vec, v_vec):
    nfeat, nr = lax.axis_size("feat"), lax.axis_size("rows")
    nz = nr // 2
    fi, ri = lax.axis_index("feat"), lax.axis_index("rows")
    ci, zi = ri % 2, ri // 2
    idx = jnp.stack([ci, fi, zi]).astype(jnp.int32)
    M, tok, fl = features.shape
    T, F = tok // nfeat, fl * nfeat
    nf = -(-(F + 3) // 8) * 8
    Dl = w_attn.shape[0]
    D = Dl * nr
    n, q = T // nr, Dl // nfeat
    WA, WB = 3 * D + 128, 5 * D
    over_feat = lambda x: [x] + [peer(x, "feat", nfeat, k) for k in range(1, nfeat)]
    groups = [[2 * z + c for z in range(nz)] for c in range(2)]
    over_z = lambda x: [x] + [peer(x, "rows", nr, 2 * k) for k in range(1, nz)]
    to_z = lambda xs: [xs[0]] + [peer(xs[k], "rows", nr, 2 * k) for k in range(1, nz)]
    to_feat = lambda xs: [xs[0]] + [peer(xs[k], "feat", nfeat, k) for k in range(1, nfeat)]
    swap_z = lambda x: lax.all_to_all(x, "rows", 0, 0, axis_index_groups=groups, tiled=True)
    swap_feat = lambda x: lax.all_to_all(x, "feat", 0, 0, tiled=True)
    over_core = lambda x: peer(x, "rows", nr, 1)

    by_quarters = q % 16 == 0
    part_rows = q if by_quarters else Dl
    pack = call(
        functools.partial(pack_kernel, WA), shape((part_rows, WA + WB), bf16), idx, *[keep_far(a) for a in (w_attn, w_ffn, w_enc.T, vectors)],
        name="pack", flops=3 * 10**9, specs=[SMEM] + [HBM] * 4,
        scratch=[pltpu.VMEM(a, f32) for a in ((part_rows, 4 * D), (part_rows, 4 * D), w_enc.T.shape, vectors.shape)] + [pltpu.VMEM((Dl, 128), f32), pltpu.SemaphoreType.DMA((4,))],
    )
    order = send_order.reshape(M, nz, 2, n)
    order_mine = jnp.where(ci == 0, order[:, :, 0], order[:, :, 1]).reshape(M, 1, T // 2)
    order_other = jnp.where(ci == 0, order[:, :, 1], order[:, :, 0]).reshape(M, 1, T // 2)
    order_theirs = over_core(order_other)
    mask = feat_mask.transpose(2, 0, 1)
    feats = tie(features, pack).transpose(2, 0, 1)
    xs = []
    for k in range(nfeat):
        part = lambda a: lax.dynamic_slice_in_dim(a, (fi ^ k) * T, T, 2)
        xs.append((part(feats) * part(mask).astype(bf16)).transpose(1, 0, 2))
    xs = to_feat(xs)
    if by_quarters:
        pa, pb = call(join_kernel, [shape((nfeat, nz, q, WA), bf16), shape((nz, q, WB), bf16)], idx, *over_z(pack), smem=1, name="join", flops=10**9)
        pa = swap_feat(pa)
    xs = xs + [over_core(x) for x in xs]
    ys = call(
        functools.partial(sort_kernel, nfeat), [shape((2, M, nf, n), bf16)] * nz, idx, order_mine, order_theirs, *xs,
        smem=1, scratch=[pltpu.VMEM((nf, T), f32), pltpu.VMEM((nz, nf, n), bf16)], name="sort", flops=3 * 10**9,
    )
    own = ys[0]
    ys = to_z(ys)
    if by_quarters:
        pa = tie(pa, *ys[1:])
        pa = [pa, over_core(pa)]
        pb = over_feat(tie(pb, own))
    else:
        pa = [lax.all_gather(pack[:, :WA], "rows", axis=0, tiled=True)]
        pb = [lax.all_gather(pack[:, WA:], "rows", axis=0, tiled=True)]

    Q = T // 4
    dma = lambda k: pltpu.SemaphoreType.DMA((k,))
    ram = lambda d, *r: pltpu.VMEM(r, d)
    vec, h, o, qkv, ext, wa, x = call(
        functools.partial(attend_kernel, nz),
        [far((8, D), f32), far((M, T, D), bf16), far((M, T, D), bf16), far((M, T, 3 * D), bf16), far((M, T, 128), bf16), far((D, WA), bf16), far((nr, M, nf, n), bf16)],
        idx, segment, context, *ys, *pa,
        smem=2, name="attend", flops=16 * 10**9, mib=36, outs=[VMEM] + [HBM] * 6,
        scratch=[ram(bf16, M, T, D), ram(bf16, M, T, D), ram(bf16, M, T, 3 * D), ram(bf16, M, T, 128), ram(bf16, D, WA), ram(bf16, 128, D), ram(bf16, T, 128), ram(f32, 4, Q, Q), ram(bf16, 2, BIG * Q, BIG * Q), dma(nz + 2 + 3 * M)],
    )

    if by_quarters:
        pb = [pb[0]] + [tie(a, o) for a in pb[1:]]
        pb = pb + [over_core(a) for a in pb]
    ng = nfeat if by_quarters else 1
    *grads_b, act, da, do, dext, gv = call(
        functools.partial(feed_kernel, len(pb), ng),
        [far((nr, q, WB) if by_quarters else (D, WB), bf16)] * ng
        + [far((M, 1, T, D), f32), far((M * T, D), bf16), far((M, T, D), bf16), far((M, T, 128), bf16), far((8, D), f32)],
        idx, keep_far(vec), *[keep_far(a) for a in (h, o, cotangent)], *pb,
        name="feed", flops=29 * 10**9, mib=56, specs=[SMEM, VMEM] + [HBM] * 3 + [VMEM] * len(pb), outs=[HBM] * (ng + 4) + [VMEM],
        scratch=[ram(bf16, M, T, D), ram(bf16, M, T, D), ram(bf16, M * T, D), ram(bf16, M, T, D), ram(bf16, M, T, 128), ram(bf16, *((nr, nfeat, q, WB) if by_quarters else (D, WB))), ram(bf16, D, WB), ram(bf16, M, 1, T, D), ram(bf16, M * T, D), ram(bf16, M * T, 2 * D), ram(bf16, M * T, D), ram(bf16, M * T, 2 * D), ram(f32, 2, T // 2, D), dma(3 * ng + 11 * M)],
    )
    if by_quarters:
        grads_b = to_feat(grads_b)
    else:
        sum_b = lax.psum_scatter(grads_b[0], "rows", scatter_dimension=0, tiled=True)

    *dxs, keep_a, send_a = call(
        functools.partial(back_kernel, nz),
        [shape((2, M, nf, n), bf16)] * nz + [shape((nz, Dl, WA), bf16)] * 2,
        idx, segment, context, keep_far(gv), *[keep_far(a) for a in (do, dext, da, qkv, ext, h, wa, x)],
        name="back", flops=29 * 10**9, mib=50, specs=[SMEM] * 2 + [VMEM] * 2 + [HBM] * 8,
        scratch=[ram(bf16, M, T, D), ram(bf16, M, T, 128), ram(bf16, M * T, D), ram(bf16, M, T, 3 * D), ram(bf16, M, T, 128), ram(bf16, M, T, D), ram(bf16, D, WA), ram(bf16, nr, M, nf, n), ram(bf16, M * T, 3 * D),
            ram(bf16, HEADS, T, 128), ram(bf16, HEADS, Q, 128), ram(f32, 4, Q, Q), ram(bf16, 2, BIG * Q, BIG * Q), ram(bf16, 2, BIG * Q, BIG * Q),
            ram(f32, D, 3 * D), ram(f32, D, 128), ram(bf16, M * T, D), dma(4 + 4 * M)],
    )

    got_a = over_core(send_a)
    if by_quarters:
        grads_b[0] = tie(grads_b[0], keep_a)
        keep_b, send_b = call(feat_b_kernel, [shape((nz, q, WB), bf16)] * 2, idx, *grads_b, smem=1, name="feat_sum_b", flops=10**9)
        got_b = over_core(send_b)
        keep_a = tie(keep_a, keep_b)
    part = call(core_kernel, shape((nfeat, nz, q, WA), bf16), keep_a, got_a, name="core_sum", flops=10**9)
    if by_quarters:
        sums = call(core_b_kernel, [shape((q, WB), bf16)] * nz, idx, tie(keep_b, part), got_b, smem=1, name="core_sum_b", flops=10**9)
        dxs[0] = tie(dxs[0], *sums)
    else:
        dxs[0] = tie(dxs[0], part)
        sums = to_feat(call(cut_kernel, [shape((q, WB), bf16)] * nfeat, idx, tie(sum_b, part), smem=1, name="cut", flops=10**9))
    dxs[1:] = [tie(a, part) for a in dxs[1:]]
    dxs = to_z(dxs)
    part = swap_feat(part)
    mine, other = call(pick_kernel, [shape((nz, M, nf, n), bf16)] * 2, idx, *dxs, smem=1, name="pick", flops=10**9)
    dx = call(
        unsort_kernel, shape((nfeat, M, fl, T), bf16), order_mine, order_other, mine, over_core(other),
        scratch=[pltpu.VMEM((nf, T), f32)], name="unsort", flops=3 * 10**9,
    )
    part = tie(part, dx)
    dx = swap_feat(dx)
    beside, sums = (sums, []) if by_quarters else ([], sums)
    part = to_z(call(functools.partial(feat_kernel, len(beside)), [shape((q, WA + len(beside) // nz * WB), bf16)] * nz, idx, part, *beside, smem=1, name="feat_sum", flops=10**9))
    grads = over_feat(call(functools.partial(rows_kernel, nz), shape((q, WA + WB), bf16), *part, *sums, name="rows_sum", flops=10**9))
    x_grad = dx.transpose(2, 1, 0, 3).reshape(fl, M, tok).astype(f32) * mask.astype(f32)
    state = [w_enc.T, m_enc.T, v_enc.T, w_attn, m_attn, v_attn, w_ffn, m_ffn, v_ffn, vectors, m_vec, v_vec]
    far_state = [keep_far(a) if a.size < Dl * D else a for a in state]
    new = call(
        functools.partial(adam_kernel, nfeat), [far(a.shape, f32) for a in state], idx, *grads, *far_state,
        specs=[SMEM] + [VMEM] * nfeat + [HBM if a.size < Dl * D else VMEM for a in state], outs=[HBM] * 12, scratch=[pltpu.VMEM(a.shape, f32) for a in state] + [pltpu.VMEM((Dl, WA + WB), f32), dma(18)], name="adamw", flops=4 * 10**9,
    )
    return (act, x_grad.transpose(1, 2, 0), *[x.T for x in new[:3]], *new[3:])


def solution(mesh):
    tok, grp = P(None, "rows", "feat"), P(None, "feat", "rows", None)
    col, row = P(None, "rows"), P("rows", None)
    return jax.shard_map(
        body,
        mesh=mesh,
        in_specs=(tok, tok, P(None, "rows", "feat", None), grp, grp, grp, col, row, row, col, col, col, row, row, row, row, col, col),
        out_specs=(grp, tok) + (col,) * 3 + (row,) * 6 + (col,) * 3,
        check_vma=False,
    )
```

```python
import functools
import math

import jax
import jax.numpy as jnp
from jax import lax
from jax.experimental import pallas as pl
from jax.experimental.pallas import tpu as pltpu
from jax.sharding import PartitionSpec as P

bf16 = jnp.bfloat16
f32 = jnp.float32
HEADS = 4
STEP = 10
BIG = 3
LN2 = math.log(2.0)
LOG2E = math.log2(math.e)
SMEM = pl.BlockSpec(memory_space=pltpu.SMEM)
VMEM = pl.BlockSpec(memory_space=pltpu.VMEM)
HBM = pl.BlockSpec(memory_space=pltpu.HBM)


def dot(a, b, ca, cb):
    return lax.dot_general(a, b, (((ca,), (cb,)), ((), ())), preferred_element_type=f32)


def nn(a, b):
    return dot(a, b, 1, 0)


def nt(a, b):
    return dot(a, b, 1, 1)


def tn(a, b):
    return dot(a, b, 0, 0)


def lanes(shape):
    return lax.broadcasted_iota(jnp.int32, shape, 1)


def subl(shape):
    return lax.broadcasted_iota(jnp.int32, shape, 0)


def split3(x):
    a = x.astype(bf16).astype(f32)
    r = x - a
    b = r.astype(bf16).astype(f32)
    return a, b, r - b


def call(kernel, out_shape, *args, smem=0, scratch=(), name=None, flops=10**6, moved=10**6, mib=16, specs=None, outs=None):
    single = not isinstance(out_shape, (list, tuple))
    return pl.pallas_call(
        kernel,
        out_shape=out_shape,
        in_specs=specs or [SMEM] * smem + [VMEM] * (len(args) - smem),
        out_specs=outs or (VMEM if single else [VMEM] * len(out_shape)),
        scratch_shapes=list(scratch),
        compiler_params=pltpu.CompilerParams(vmem_limit_bytes=mib << 20),
        cost_estimate=pl.CostEstimate(flops=flops, bytes_accessed=moved, transcendentals=0),
        name=name,
    )(*args)


def shape(s, d):
    return jax.ShapeDtypeStruct(tuple(s), d)


def far(s, d):
    return pltpu.HBM(tuple(s), d)


def keep_far(x):
    return pltpu.with_memory_space_constraint(x, pltpu.HBM)


class Copies:
    def __init__(self, sems):
        self.sems, self.used, self.open = sems, 0, {}

    def start(self, key, src, dst):
        self.open[key] = pltpu.make_async_copy(src, dst, self.sems.at[self.used])
        self.used += 1
        self.open[key].start()

    def wait(self, key):
        if key in self.open:
            self.open.pop(key).wait()

    def wait_all(self):
        for key in list(self.open):
            self.wait(key)


CORE, FEAT, ZED = 0, 1, 2


def starts(seg_ref, m, T):
    q = T // 4
    first = seg_ref[m, 0, 0, 0] == seg_ref[m, 0, 0, q]
    big = jnp.where(first, 0, q)
    small = jnp.where(first, 3 * q, 0)
    return pl.multiple_of(big, q), pl.multiple_of(small, q)


def neighbourhoods(seg_ref, m, T):
    q = T // 4
    big, small = starts(seg_ref, m, T)
    for base, nb in ((big, BIG), (small, 4 - BIG)):
        yield base, nb, [pl.multiple_of(base + b * q, q) for b in range(nb)]


def split_rows(acc, core, keep_ref, send_ref, cols):
    nz, dl = keep_ref.shape[0], keep_ref.shape[1]
    for z in range(nz):
        mine = pl.multiple_of((2 * z + core) * dl, 8)
        other = pl.multiple_of((2 * z + 1 - core) * dl, 8)
        keep_ref[z, :, cols] = acc[pl.ds(mine, dl), :].astype(bf16)
        send_ref[z, :, cols] = acc[pl.ds(other, dl), :].astype(bf16)


def pack_kernel(WA, idx_ref, attn_ref, ffn_ref, enc_ref, vec_ref, out_ref, attn_s, ffn_s, enc_s, vec_s, x_s, sems):
    D3, Dl, q = WA - 128, enc_s.shape[0], out_ref.shape[0]
    D = D3 // 3
    rows = slice(None) if q == Dl else pl.ds(pl.multiple_of(idx_ref[FEAT] * q, q), q)
    copies = Copies(sems)
    for key, src, dst in (("e", enc_ref, enc_s), ("v", vec_ref, vec_s), ("a", attn_ref.at[rows, :], attn_s), ("f", ffn_ref.at[rows, :], ffn_s)):
        copies.start(key, src, dst)
    copies.wait("e")
    copies.wait("v")
    p = split3(vec_s[...])
    none = jnp.zeros((1, Dl), f32)
    t = jnp.concatenate([x[0:1] for x in p] + [none] + [x[1:6] for x in p] + [jnp.zeros((9, Dl), f32)], axis=0)
    x_s[...] = jnp.concatenate([enc_s[...], t.T], axis=1)
    out_ref[:, D3:WA] = x_s[rows, :].astype(bf16)
    copies.wait("a")
    out_ref[:, 0:D3] = attn_s[:, 0:D3].astype(bf16)
    out_ref[:, WA : WA + D] = attn_s[:, D3:].astype(bf16)
    copies.wait("f")
    out_ref[:, WA + D :] = ffn_s[...].astype(bf16)


def join_kernel(idx_ref, *refs):
    a_ref, b_ref = refs[-2:]
    A = a_ref.shape[3]
    for j, ref in enumerate(refs[:-2]):
        z = idx_ref[ZED] ^ j
        b_ref[z] = ref[:, A:]
        for g in range(a_ref.shape[0]):
            a_ref[g, z] = ref[:, 0:A]


def assemble(idx_ref, pieces, dst):
    if len(pieces) == 1:
        dst[...] = pieces[0][...]
        return
    if len(pieces) == 2:
        nfeat, nz, q, _ = pieces[0].shape
        for c in range(2):
            for g in range(nfeat):
                for j in range(nz):
                    r = (j * 2 + (idx_ref[CORE] ^ c)) * (nfeat * q) + g * q
                    dst[pl.ds(pl.multiple_of(r, q), q), :] = pieces[c][g, j]
        return
    nz, q, _ = pieces[0].shape
    nfeat = len(pieces) // 2
    for c in range(2):
        for k in range(nfeat):
            for j in range(nz):
                r = (j * 2 + (idx_ref[CORE] ^ c)) * (nfeat * q) + (idx_ref[FEAT] ^ k) * q
                dst[pl.ds(pl.multiple_of(r, q), q), :] = pieces[c * nfeat + k][j]


def one_hot(order, T):
    return jnp.where(subl((T, order.shape[1])) == order, 1.0, 0.0).astype(bf16)


def sort_kernel(nfeat, idx_ref, mine_ref, theirs_ref, *refs):
    xs, outs, s_ref, y_ref = refs[: 2 * nfeat], refs[2 * nfeat : -2], refs[-2], refs[-1]
    M, f, T = xs[0].shape
    nz, nf, n = y_ref.shape
    s_ref[nfeat * f :, :] = jnp.where(subl((nf - nfeat * f, T)) < 3, 1.0, 0.0)
    for s, order_ref in enumerate((mine_ref, theirs_ref)):
        core = idx_ref[CORE] ^ s
        for m in range(M):
            for k in range(nfeat):
                for g in range(nfeat):

                    @pl.when((idx_ref[FEAT] ^ k) == g)
                    def _():
                        s_ref[g * f : (g + 1) * f, :] = xs[s * nfeat + k][m].astype(f32)

            y = nn(s_ref[...].astype(bf16), one_hot(order_ref[m], T)).astype(bf16)
            for z in range(nz):
                y_ref[z] = y[:, z * n : (z + 1) * n]
            for j, out in enumerate(outs):
                out[core, m] = y_ref[idx_ref[ZED] ^ j]


def pick_kernel(idx_ref, *refs):
    mine_ref, other_ref = refs[-2:]
    for j, ref in enumerate(refs[:-2]):
        mine_ref[idx_ref[ZED] ^ j] = ref[idx_ref[CORE]]
        other_ref[idx_ref[ZED] ^ j] = ref[1 - idx_ref[CORE]]


def unsort_kernel(mine_ref, other_ref, x_ref, got_ref, out_ref, s_ref):
    nz = x_ref.shape[0]
    nfeat, M, f, T = out_ref.shape
    for m in range(M):
        mine = jnp.concatenate([x_ref[z, m] for z in range(nz)], axis=1)
        other = jnp.concatenate([got_ref[z, m] for z in range(nz)], axis=1)
        s_ref[...] = nt(mine, one_hot(mine_ref[m], T)) + nt(other, one_hot(other_ref[m], T))
        for g in range(nfeat):
            out_ref[g, m] = s_ref[g * f : (g + 1) * f, :].astype(bf16)


def attend_kernel(nz, idx_ref, seg_ref, ctx_ref, *refs):
    ys, refs = refs[:nz], refs[nz:]
    pieces, refs = refs[:-17], refs[-17:]
    vec_ref, h_out, o_out, qkv_out, ext_out, wa_out, x_out, h_ref, o_ref, qkv_ref, ext_ref, wa_ref, wev_ref, kext_s, diag_s, e_s, sems = refs
    M, T, D = h_ref.shape
    Q, HD = T // 4, D // HEADS
    nf, n = ys[0].shape[2], ys[0].shape[3]
    copies = Copies(sems)
    for j in range(nz):
        copies.start(("x", j), ys[j], x_out.at[pl.ds(2 * (idx_ref[ZED] ^ j), 2)])
    assemble(idx_ref, pieces, wa_ref)
    copies.start("wa", wa_ref, wa_out)
    t = wa_ref[:, 3 * D :].astype(f32).T
    wev_ref[...] = t.astype(bf16)
    vec_ref[...] = jnp.concatenate([jnp.zeros((1, D), f32), t[104:109] + t[109:114] + t[114:119], jnp.zeros((2, D), f32)], axis=0)
    wev = wev_ref[0:nf, :]
    c = LOG2E * HD**-0.5
    qext = jnp.where(lanes((Q, 128)) == 0, 1.0, 0.0).astype(bf16)
    lane = lanes((Q, 128))
    for m in range(M):
        for j in range(nz):
            for s in range(2):
                r = pl.multiple_of(((idx_ref[ZED] ^ j) * 2 + s) * n, n)
                h_ref[m, pl.ds(r, n), :] = tn(ys[j][s, m], wev).astype(bf16)
    copies.start("h", h_ref, h_out)
    for m in range(M):
        h = h_ref[m]
        qkv_ref[m, :, 0:D] = (nn(h, wa_ref[:, 0:D]) * c).astype(bf16)
        qkv_ref[m, :, D : 3 * D] = nn(h, wa_ref[:, D : 3 * D]).astype(bf16)
        copies.start(("qkv", m), qkv_ref.at[m], qkv_out.at[m])
        bias = jnp.where(ctx_ref[m, 0] == 1, 0.0, -1e30).astype(f32)
        bcol = jnp.broadcast_to(bias, (128, T)).T
        kext_s[...] = jnp.where(lanes((T, 128)) == 0, bcol, 0.0).astype(bf16)
        for b in range(4):
            row = jnp.broadcast_to(bias[:, b * Q : (b + 1) * Q], (Q, Q))
            diag_s[b] = jnp.where(subl((Q, Q)) == lanes((Q, Q)), 0.0, row)
        for base, nb, rows in neighbourhoods(seg_ref, m, T):
            every = pl.ds(base, nb * Q)
            exts = [jnp.where(lane == 12, 1.0, 0.0) for _ in range(nb)]
            for hd in range(HEADS):
                cq = slice(hd * HD, (hd + 1) * HD)
                ck = slice(D + hd * HD, D + (hd + 1) * HD)
                cv = slice(2 * D + hd * HD, 2 * D + (hd + 1) * HD)
                tops = []
                for qb in range(nb):
                    q = qkv_ref[m, pl.ds(rows[qb], Q), cq]
                    qa = jnp.concatenate([q, qext], axis=1)
                    s = []
                    for kb in range(nb):
                        k = qkv_ref[m, pl.ds(rows[kb], Q), ck]
                        if kb == qb:
                            s.append(nt(q, k) + diag_s[rows[kb] // Q])
                        else:
                            s.append(nt(qa, jnp.concatenate([k, kext_s[pl.ds(rows[kb], Q), :]], axis=1)))
                    top = jnp.max(functools.reduce(jnp.maximum, s), axis=1, keepdims=True)
                    tops.append(top)
                    for kb in range(nb):
                        e_s[hd % 2, qb * Q : (qb + 1) * Q, kb * Q : (kb + 1) * Q] = jnp.exp2(s[kb] - top).astype(bf16)
                v = qkv_ref[m, every, cv]
                acc = nn(e_s[hd % 2, 0 : nb * Q, 0 : nb * Q], jnp.concatenate([v, jnp.ones((nb * Q, 128), bf16)], axis=1))
                total = acc[:, HD:]
                o_ref[m, every, cq] = (acc[:, :HD] / total).astype(bf16)
                for qb in range(nb):
                    lse = tops[qb] + jnp.log2(total[qb * Q : (qb + 1) * Q])
                    for j, part in enumerate(split3(lse)):
                        exts[qb] = jnp.where(lane == 3 * hd + j, part, exts[qb])
            for qb in range(nb):
                ext_ref[m, pl.ds(rows[qb], Q), :] = exts[qb].astype(bf16)
        copies.start(("ext", m), ext_ref.at[m], ext_out.at[m])
        copies.start(("o", m), o_ref.at[m], o_out.at[m])
    copies.wait_all()


def gelu_parts(u):
    cdf = 0.5 + 0.5 * lax.erf(u * (2.0**-0.5))
    pdf = jnp.exp2(u * u * (-0.5 * LOG2E)) * (1.0 / math.sqrt(2.0 * math.pi))
    return cdf, pdf


def colsum(x):
    return jnp.sum(x.reshape(x.shape[0] // 8, 8, x.shape[1]), axis=0)


def mean(x):
    return jnp.mean(x, axis=1, keepdims=True)


def feed_kernel(np_, ng, idx_ref, vec_ref, h_hbm, o_hbm, cot_hbm, *refs):
    pieces, refs = refs[:np_], refs[np_:]
    gb_outs, refs = refs[:ng], refs[ng:]
    act_ref, da_out, do_out, dext_out, gv_ref, h_ref, o_ref, da_ref, do_ref, dext_ref, gb_ref, wb_s, cot_ref, y1_s, gr_s, db_s, du_s, act_s, sems = refs
    M, T, D = h_ref.shape
    F, HD, B = 2 * D, D // HEADS, T // 2
    wo, w1, w2 = slice(0, D), slice(D, D + F), slice(D + F, D + 2 * F)
    copies = Copies(sems)
    for m in range(M):
        copies.start(("o", m), o_hbm.at[m], o_ref.at[m])
        copies.start(("h", m), h_hbm.at[m], h_ref.at[m])
        copies.start(("cot", m), cot_hbm.at[m], cot_ref.at[m])
    assemble(idx_ref, pieces, wb_s)
    g1, s1, g2, s2, b2 = (vec_ref[j : j + 1, :] for j in range(1, 6))
    lane = lanes((B, 128))
    vsum = [0.0] * 5

    def chain(m, b):
        r = slice(b * B, (b + 1) * B)
        w = slice(m * T + b * B, m * T + (b + 1) * B)
        copies.wait(("o", m))
        o = o_ref[m, r, :]
        t = nn(o, wb_s[:, wo])
        yield
        copies.wait(("h", m))
        a = h_ref[m, r, :].astype(f32) + t
        ac = a - mean(a)
        i1 = lax.rsqrt(mean(ac * ac) + 1e-5)
        xh1 = ac * i1
        y1 = xh1 * g1 + s1
        y1b = y1.astype(bf16)
        y1_s[w, :] = y1b
        u = nn(y1b, wb_s[:, w1])
        yield
        cdf, pdf = gelu_parts(u)
        gr = (u * cdf).astype(bf16)
        gr_s[w, :] = gr
        dgelu = cdf + u * pdf
        t = nt(gr, wb_s[:, w2])
        yield
        z = y1 + t + b2
        zc = z - mean(z)
        i2 = lax.rsqrt(mean(zc * zc) + 1e-5)
        xh2 = zc * i2
        copies.wait(("act", b))
        act_s[b] = xh2 * g2 + s2
        copies.start(("act", b), act_s.at[b], act_ref.at[m, 0, pl.ds(b * B, B), :])
        copies.wait(("cot", m))
        c = cot_ref[m, 0, r, :].astype(f32)
        vsum[2] += colsum(c * xh2)
        vsum[3] += colsum(c)
        cg = c * g2
        db = i2 * (cg - mean(cg) - xh2 * mean(cg * xh2))
        vsum[4] += colsum(db)
        dbr = db.astype(bf16)
        db_s[w, :] = dbr
        t = nn(dbr, wb_s[:, w2])
        yield
        du = (t * dgelu).astype(bf16)
        du_s[w, :] = du
        t = nt(du, wb_s[:, w1])
        yield
        dy = db + t
        vsum[0] += colsum(dy * xh1)
        vsum[1] += colsum(dy)
        cg = dy * g1
        da = i1 * (cg - mean(cg) - xh1 * mean(cg * xh1))
        dar = da.astype(bf16)
        da_ref[w, :] = dar
        do = nt(dar, wb_s[:, wo]).astype(bf16)
        yield
        do_ref[m, r, :] = do
        od = o.astype(f32) * do.astype(f32)
        ext = jnp.zeros((B, 128), f32)
        for hd in range(HEADS):
            delta = jnp.sum(od[:, hd * HD : (hd + 1) * HD], axis=1, keepdims=True)
            for j, part in enumerate(split3(delta)):
                ext = jnp.where(lane == 3 * hd + j, part, ext)
        dext_ref[m, r, :] = ext.astype(bf16)
        copies.start(("da", m, b), da_ref.at[w, :], da_out.at[w, :])
        copies.start(("do", m, b), do_ref.at[m, r, :], do_out.at[m, r, :])
        copies.start(("dext", m, b), dext_ref.at[m, r, :], dext_out.at[m, r, :])

    for m in range(M):
        gens = [chain(m, b) for b in range(2)]
        for _ in range(7):
            for g in gens:
                next(g, None)
    gv_ref[...] = jnp.concatenate([jnp.zeros((1, D), f32)] + [jnp.sum(x, axis=0, keepdims=True) for x in vsum] + [jnp.zeros((2, D), f32)], axis=0)
    left = {wo.start: (o_ref[...].reshape(M * T, D), da_ref), w1.start: (y1_s, du_s), w2.start: (db_s, gr_s)}
    for cols in (w2, w1, wo):
        a, b = left[cols.start]
        g = tn(a[...], b[...]).astype(bf16)
        if ng == 1:
            gb_ref[:, cols] = g
            copies.start(("gb", cols.start), gb_ref.at[:, cols], gb_outs[0].at[:, cols])
        else:
            nr, q, _ = gb_outs[0].shape
            gb_ref[:, :, :, cols] = g.reshape(nr, ng, q, g.shape[1])
            for k, out in enumerate(gb_outs):
                copies.start(("gb", cols.start, k), gb_ref.at[:, idx_ref[FEAT] ^ k, :, cols], out.at[:, :, cols])
    copies.wait_all()


def back_kernel(nz, idx_ref, seg_ref, ctx_ref, gv_ref, do_hbm, dext_hbm, da_hbm, qkv_hbm, ext_hbm, h_hbm, wa_hbm, x_hbm, *refs):
    outs, refs = refs[:nz], refs[nz:]
    keep_ref, send_ref, do_ref, dext_ref, da_ref, qkv_ref, ext_ref, h_ref, wa_ref, x_ref, dqkv_s, kb_s, ku_s, diag_s, p_s, ds_s, acc_s, accx_s, dh_s, sems = refs
    M, T, D = do_ref.shape
    Q, HD = T // 4, D // HEADS
    nf, n = x_ref.shape[2], x_ref.shape[3]
    scale = HD**-0.5
    copies = Copies(sems)
    for m in range(M):
        for key, src, dst in (("ext", ext_hbm, ext_ref), ("qkv", qkv_hbm, qkv_ref), ("dext", dext_hbm, dext_ref), ("do", do_hbm, do_ref)):
            copies.start((key, m), src.at[m], dst.at[m])
    for key, src, dst in (("da", da_hbm, da_ref), ("h", h_hbm, h_ref), ("wa", wa_hbm, wa_ref), ("x", x_hbm, x_ref)):
        copies.start(key, src, dst)
    lane = lanes((T, 128))
    for m in range(M):
        bias = jnp.where(ctx_ref[m, 0] == 1, 0.0, -1e30).astype(f32)
        bcol = jnp.broadcast_to(bias, (128, T)).T
        for hd in range(HEADS):
            un = jnp.where((lane >= 3 * hd) & (lane < 3 * hd + 3), -1.0, 0.0)
            if m == 0:
                ku_s[hd] = un[:Q].astype(bf16)
            kb_s[hd] = jnp.where(lane == 12, bcol, un).astype(bf16)
        for b in range(4):
            col = bcol[b * Q : (b + 1) * Q, 0:1]
            diag_s[b] = jnp.where(subl((Q, Q)) == lanes((Q, Q)), 0.0, jnp.broadcast_to(col, (Q, Q)))
        for key in ("ext", "qkv", "dext", "do"):
            copies.wait((key, m))
        for base, nb, rows in neighbourhoods(seg_ref, m, T):
            every = pl.ds(base, nb * Q)
            out = pl.ds(pl.multiple_of(m * T + base, Q), nb * Q)
            w = nb * Q
            for hd in range(HEADS):
                cq = slice(hd * HD, (hd + 1) * HD)
                ck = slice(D + hd * HD, D + (hd + 1) * HD)
                cv = slice(2 * D + hd * HD, 2 * D + (hd + 1) * HD)
                for qb in range(nb):
                    here = pl.ds(rows[qb], Q)
                    qa = jnp.concatenate([qkv_ref[m, here, cq], ext_ref[m, here, :]], axis=1)
                    da = jnp.concatenate([do_ref[m, here, cq], dext_ref[m, here, :]], axis=1)
                    for kb in range(nb):
                        k = qkv_ref[m, pl.ds(rows[kb], Q), ck]
                        v = qkv_ref[m, pl.ds(rows[kb], Q), cv]
                        if kb == qb:
                            s = nt(jnp.concatenate([k, ku_s[hd]], axis=1), qa) + diag_s[rows[kb] // Q]
                        else:
                            s = nt(jnp.concatenate([k, kb_s[hd, pl.ds(rows[kb], Q), :]], axis=1), qa)
                        p = jnp.exp2(s)
                        dp = nt(jnp.concatenate([v, ku_s[hd]], axis=1), da)
                        p_s[hd % 2, kb * Q : (kb + 1) * Q, qb * Q : (qb + 1) * Q] = p.astype(bf16)
                        ds_s[hd % 2, kb * Q : (kb + 1) * Q, qb * Q : (qb + 1) * Q] = (p * dp).astype(bf16)
                p, ds = p_s[hd % 2, 0:w, 0:w], ds_s[hd % 2, 0:w, 0:w]
                dqkv_s[out, cv] = nn(p, do_ref[m, every, cq]).astype(bf16)
                dqkv_s[out, ck] = (nn(ds, qkv_ref[m, every, cq]) * LN2).astype(bf16)
                dqkv_s[out, cq] = (tn(qkv_ref[m, every, ck], ds) * scale).T.astype(bf16)
    for key in ("wa", "x", "da"):
        copies.wait(key)
    wev = wa_ref[:, 3 * D :].astype(f32).T.astype(bf16)[0:nf, :]
    dh_s[...] = (da_ref[...].astype(f32) + nt(dqkv_s[...], wa_ref[:, 0 : 3 * D])).astype(bf16)
    e = None
    for m in range(M):
        for j in range(nz):
            for s in range(2):
                r = (idx_ref[ZED] ^ j) * 2 + s
                dh = dh_s[pl.ds(pl.multiple_of(m * T + r * n, n), n), :]
                outs[j][s, m] = nt(wev, dh).astype(bf16)
                t = nn(x_ref[r, m], dh)
                e = t if e is None else e + t
    rest = jnp.concatenate([e[100:101], gv_ref[1:6, :], jnp.zeros((128 - nf - 6, D), f32)], axis=0)
    accx_s[...] = jnp.concatenate([e, rest], axis=0).T
    core = idx_ref[CORE]
    split_rows(accx_s, core, keep_ref, send_ref, slice(3 * D, 3 * D + 128))
    copies.wait("h")
    g = tn(h_ref[...].reshape(M * T, D), dqkv_s[...])
    if len(acc_s.shape) == 3:
        acc_s[...] = g.astype(bf16).reshape(acc_s.shape)
        for z in range(keep_ref.shape[0]):
            keep_ref[z, :, 0 : 3 * D] = acc_s[2 * z + core]
            send_ref[z, :, 0 : 3 * D] = acc_s[2 * z + 1 - core]
    else:
        acc_s[...] = g
        split_rows(acc_s, core, keep_ref, send_ref, slice(0, 3 * D))


def core_kernel(keep_ref, got_ref, out_ref):
    nfeat, _, q, _ = out_ref.shape
    for g in range(nfeat):
        rows = slice(g * q, (g + 1) * q)
        out_ref[g] = (keep_ref[:, rows, :].astype(f32) + got_ref[:, rows, :].astype(f32)).astype(bf16)


def feat_kernel(na, idx_ref, a_ref, *refs):
    bs, outs = refs[:na], refs[na:]
    A = a_ref.shape[3]
    for j, out in enumerate(outs):
        out[:, 0:A] = sum(a_ref[g, idx_ref[ZED] ^ j].astype(f32) for g in range(a_ref.shape[0])).astype(bf16)
        if bs:
            out[:, A:] = bs[j][...]


def cut_kernel(idx_ref, x_ref, *outs):
    q = outs[0].shape[0]
    for g in range(len(outs)):
        for k, out in enumerate(outs):

            @pl.when((idx_ref[FEAT] ^ k) == g)
            def _():
                out[...] = x_ref[g * q : (g + 1) * q, :]


def feat_b_kernel(idx_ref, *refs):
    keep_ref, send_ref = refs[-2:]
    for z in range(keep_ref.shape[0]):
        for c, out in ((idx_ref[CORE], keep_ref), (1 - idx_ref[CORE], send_ref)):
            out[z] = sum(x[2 * z + c].astype(f32) for x in refs[:-2]).astype(bf16)


def core_b_kernel(idx_ref, keep_ref, got_ref, *outs):
    for j, out in enumerate(outs):
        z = idx_ref[ZED] ^ j
        out[...] = (keep_ref[z].astype(f32) + got_ref[z].astype(f32)).astype(bf16)


def rows_kernel(na, *refs):
    out = refs[-1]
    W = refs[0].shape[1]
    out[:, 0:W] = sum(x[...].astype(f32) for x in refs[:na]).astype(bf16)
    if len(refs) > na + 1:
        out[:, W:] = sum(x[...].astype(f32) for x in refs[na:-1]).astype(bf16)


def update(w, g, m, v, rate):
    m = 0.9 * m + 0.1 * g
    v = 0.95 * v + 0.05 * g * g
    return w - rate * ((m / (1.0 - 0.9**STEP)) / (jnp.sqrt(v / (1.0 - 0.95**STEP)) + 1e-8) + 0.1 * w), m, v


def adam_kernel(nfeat, idx_ref, *refs):
    gs, refs = refs[:nfeat], refs[nfeat:]
    ins, outs, held, g_s, sems = refs[:12], refs[12:24], refs[24:36], refs[36], refs[37]
    copies = Copies(sems)
    small = (0, 1, 2, 9, 10, 11)
    for i in small:
        copies.start(("in", i), ins[i], held[i])
    q = gs[0].shape[0]
    for k in range(nfeat):
        for f in range(nfeat):

            @pl.when((idx_ref[FEAT] ^ k) == f)
            def _():
                g_s[f * q : (f + 1) * q, :] = gs[k][...].astype(f32)

    D = ins[3].shape[1] // 4
    F, A = ins[0].shape[1], 3 * D + 128

    def step(i, g, rate):
        state = [(held if i + j in small else ins)[i + j][...] for j in range(3)]
        for j, x in enumerate(update(state[0], g, state[1], state[2], rate)):
            held[i + j][...] = x
            copies.start(("out", i + j), held[i + j], outs[i + j])

    step(6, g_s[:, A + D :], 0.02)
    step(3, jnp.concatenate([g_s[:, 0 : 3 * D], g_s[:, A : A + D]], axis=1), 0.25)
    for i in small:
        copies.wait(("in", i))
    x = g_s[:, 3 * D : A]
    step(0, x[:, 0:F], 0.08)
    step(9, x.T[104:110, :], 0.2)
    copies.wait_all()


def peer(x, axis, size, k):
    return lax.ppermute(x, axis, [(i, i ^ k) for i in range(size)])


def tie(x, *others):
    return lax.optimization_barrier((x, *others))[0]


def body(features, feat_mask, send_order, segment, context, cotangent, w_enc, w_attn, w_ffn, vectors, m_enc, v_enc, m_attn, v_attn, m_ffn, v_ffn, m_vec, v_vec):
    nfeat, nr = lax.axis_size("feat"), lax.axis_size("rows")
    nz = nr // 2
    fi, ri = lax.axis_index("feat"), lax.axis_index("rows")
    ci, zi = ri % 2, ri // 2
    idx = jnp.stack([ci, fi, zi]).astype(jnp.int32)
    M, tok, fl = features.shape
    T, F = tok // nfeat, fl * nfeat
    nf = -(-(F + 3) // 8) * 8
    Dl = w_attn.shape[0]
    D = Dl * nr
    n, q = T // nr, Dl // nfeat
    WA, WB = 3 * D + 128, 5 * D
    over_feat = lambda x: [x] + [peer(x, "feat", nfeat, k) for k in range(1, nfeat)]
    groups = [[2 * z + c for z in range(nz)] for c in range(2)]
    over_z = lambda x: [x] + [peer(x, "rows", nr, 2 * k) for k in range(1, nz)]
    to_z = lambda xs: [xs[0]] + [peer(xs[k], "rows", nr, 2 * k) for k in range(1, nz)]
    to_feat = lambda xs: [xs[0]] + [peer(xs[k], "feat", nfeat, k) for k in range(1, nfeat)]
    swap_z = lambda x: lax.all_to_all(x, "rows", 0, 0, axis_index_groups=groups, tiled=True)
    swap_feat = lambda x: lax.all_to_all(x, "feat", 0, 0, tiled=True)
    over_core = lambda x: peer(x, "rows", nr, 1)

    by_quarters = q % 16 == 0
    part_rows = q if by_quarters else Dl
    pack = call(
        functools.partial(pack_kernel, WA), shape((part_rows, WA + WB), bf16), idx, *[keep_far(a) for a in (w_attn, w_ffn, w_enc.T, vectors)],
        name="pack", flops=3 * 10**9, specs=[SMEM] + [HBM] * 4,
        scratch=[pltpu.VMEM(a, f32) for a in ((part_rows, 4 * D), (part_rows, 4 * D), w_enc.T.shape, vectors.shape)] + [pltpu.VMEM((Dl, 128), f32), pltpu.SemaphoreType.DMA((4,))],
    )
    order = send_order.reshape(M, nz, 2, n)
    order_mine = jnp.where(ci == 0, order[:, :, 0], order[:, :, 1]).reshape(M, 1, T // 2)
    order_other = jnp.where(ci == 0, order[:, :, 1], order[:, :, 0]).reshape(M, 1, T // 2)
    order_theirs = over_core(order_other)
    mask = feat_mask.transpose(2, 0, 1)
    feats = tie(features, pack).transpose(2, 0, 1)
    xs = []
    for k in range(nfeat):
        part = lambda a: lax.dynamic_slice_in_dim(a, (fi ^ k) * T, T, 2)
        xs.append((part(feats) * part(mask).astype(bf16)).transpose(1, 0, 2))
    xs = to_feat(xs)
    if by_quarters:
        pa, pb = call(join_kernel, [shape((nfeat, nz, q, WA), bf16), shape((nz, q, WB), bf16)], idx, *over_z(pack), smem=1, name="join", flops=10**9)
        pa = swap_feat(pa)
    xs = xs + [over_core(x) for x in xs]
    ys = call(
        functools.partial(sort_kernel, nfeat), [shape((2, M, nf, n), bf16)] * nz, idx, order_mine, order_theirs, *xs,
        smem=1, scratch=[pltpu.VMEM((nf, T), f32), pltpu.VMEM((nz, nf, n), bf16)], name="sort", flops=3 * 10**9,
    )
    own = ys[0]
    ys = to_z(ys)
    if by_quarters:
        pa = tie(pa, *ys[1:])
        pa = [pa, over_core(pa)]
        pb = over_feat(tie(pb, own))
    else:
        pa = [lax.all_gather(pack[:, :WA], "rows", axis=0, tiled=True)]
        pb = [lax.all_gather(pack[:, WA:], "rows", axis=0, tiled=True)]

    Q = T // 4
    dma = lambda k: pltpu.SemaphoreType.DMA((k,))
    ram = lambda d, *r: pltpu.VMEM(r, d)
    vec, h, o, qkv, ext, wa, x = call(
        functools.partial(attend_kernel, nz),
        [far((8, D), f32), far((M, T, D), bf16), far((M, T, D), bf16), far((M, T, 3 * D), bf16), far((M, T, 128), bf16), far((D, WA), bf16), far((nr, M, nf, n), bf16)],
        idx, segment, context, *ys, *pa,
        smem=2, name="attend", flops=16 * 10**9, mib=36, outs=[VMEM] + [HBM] * 6,
        scratch=[ram(bf16, M, T, D), ram(bf16, M, T, D), ram(bf16, M, T, 3 * D), ram(bf16, M, T, 128), ram(bf16, D, WA), ram(bf16, 128, D), ram(bf16, T, 128), ram(f32, 4, Q, Q), ram(bf16, 2, BIG * Q, BIG * Q), dma(nz + 2 + 3 * M)],
    )

    if by_quarters:
        pb = [pb[0]] + [tie(a, o) for a in pb[1:]]
        pb = pb + [over_core(a) for a in pb]
    ng = nfeat if by_quarters else 1
    *grads_b, act, da, do, dext, gv = call(
        functools.partial(feed_kernel, len(pb), ng),
        [far((nr, q, WB) if by_quarters else (D, WB), bf16)] * ng
        + [far((M, 1, T, D), f32), far((M * T, D), bf16), far((M, T, D), bf16), far((M, T, 128), bf16), far((8, D), f32)],
        idx, keep_far(vec), *[keep_far(a) for a in (h, o, cotangent)], *pb,
        name="feed", flops=29 * 10**9, mib=56, specs=[SMEM, VMEM] + [HBM] * 3 + [VMEM] * len(pb), outs=[HBM] * (ng + 4) + [VMEM],
        scratch=[ram(bf16, M, T, D), ram(bf16, M, T, D), ram(bf16, M * T, D), ram(bf16, M, T, D), ram(bf16, M, T, 128), ram(bf16, *((nr, nfeat, q, WB) if by_quarters else (D, WB))), ram(bf16, D, WB), ram(bf16, M, 1, T, D), ram(bf16, M * T, D), ram(bf16, M * T, 2 * D), ram(bf16, M * T, D), ram(bf16, M * T, 2 * D), ram(f32, 2, T // 2, D), dma(3 * ng + 11 * M)],
    )
    if by_quarters:
        grads_b = to_feat(grads_b)
    else:
        sum_b = lax.psum_scatter(grads_b[0], "rows", scatter_dimension=0, tiled=True)

    *dxs, keep_a, send_a = call(
        functools.partial(back_kernel, nz),
        [shape((2, M, nf, n), bf16)] * nz + [shape((nz, Dl, WA), bf16)] * 2,
        idx, segment, context, keep_far(gv), *[keep_far(a) for a in (do, dext, da, qkv, ext, h, wa, x)],
        name="back", flops=29 * 10**9, mib=50, specs=[SMEM] * 2 + [VMEM] * 2 + [HBM] * 8,
        scratch=[ram(bf16, M, T, D), ram(bf16, M, T, 128), ram(bf16, M * T, D), ram(bf16, M, T, 3 * D), ram(bf16, M, T, 128), ram(bf16, M, T, D), ram(bf16, D, WA), ram(bf16, nr, M, nf, n), ram(bf16, M * T, 3 * D),
            ram(bf16, HEADS, T, 128), ram(bf16, HEADS, Q, 128), ram(f32, 4, Q, Q), ram(bf16, 2, BIG * Q, BIG * Q), ram(bf16, 2, BIG * Q, BIG * Q),
            ram(bf16, nr, Dl, 3 * D) if by_quarters else ram(f32, D, 3 * D), ram(f32, D, 128), ram(bf16, M * T, D), dma(4 + 4 * M)],
    )

    got_a = over_core(send_a)
    if by_quarters:
        grads_b[0] = tie(grads_b[0], keep_a)
        keep_b, send_b = call(feat_b_kernel, [shape((nz, q, WB), bf16)] * 2, idx, *grads_b, smem=1, name="feat_sum_b", flops=10**9)
        got_b = over_core(send_b)
        keep_a = tie(keep_a, keep_b)
    part = call(core_kernel, shape((nfeat, nz, q, WA), bf16), keep_a, got_a, name="core_sum", flops=10**9)
    if by_quarters:
        sums = call(core_b_kernel, [shape((q, WB), bf16)] * nz, idx, tie(keep_b, part), got_b, smem=1, name="core_sum_b", flops=10**9)
        dxs[0] = tie(dxs[0], *sums)
    else:
        dxs[0] = tie(dxs[0], part)
        sums = to_feat(call(cut_kernel, [shape((q, WB), bf16)] * nfeat, idx, tie(sum_b, part), smem=1, name="cut", flops=10**9))
    dxs[1:] = [tie(a, part) for a in dxs[1:]]
    dxs = to_z(dxs)
    part = swap_feat(part)
    mine, other = call(pick_kernel, [shape((nz, M, nf, n), bf16)] * 2, idx, *dxs, smem=1, name="pick", flops=10**9)
    dx = call(
        unsort_kernel, shape((nfeat, M, fl, T), bf16), order_mine, order_other, mine, over_core(other),
        scratch=[pltpu.VMEM((nf, T), f32)], name="unsort", flops=3 * 10**9,
    )
    part = tie(part, dx)
    dx = swap_feat(dx)
    beside, sums = (sums, []) if by_quarters else ([], sums)
    part = to_z(call(functools.partial(feat_kernel, len(beside)), [shape((q, WA + len(beside) // nz * WB), bf16)] * nz, idx, part, *beside, smem=1, name="feat_sum", flops=10**9))
    grads = over_feat(call(functools.partial(rows_kernel, nz), shape((q, WA + WB), bf16), *part, *sums, name="rows_sum", flops=10**9))
    x_grad = dx.transpose(2, 1, 0, 3).reshape(fl, M, tok).astype(f32) * mask.astype(f32)
    state = [w_enc.T, m_enc.T, v_enc.T, w_attn, m_attn, v_attn, w_ffn, m_ffn, v_ffn, vectors, m_vec, v_vec]
    far_state = [keep_far(a) if a.size < Dl * D else a for a in state]
    new = call(
        functools.partial(adam_kernel, nfeat), [far(a.shape, f32) for a in state], idx, *grads, *far_state,
        specs=[SMEM] + [VMEM] * nfeat + [HBM if a.size < Dl * D else VMEM for a in state], outs=[HBM] * 12, scratch=[pltpu.VMEM(a.shape, f32) for a in state] + [pltpu.VMEM((Dl, WA + WB), f32), dma(18)], name="adamw", flops=4 * 10**9,
    )
    return (act, x_grad.transpose(1, 2, 0), *[x.T for x in new[:3]], *new[3:])


def solution(mesh):
    tok, grp = P(None, "rows", "feat"), P(None, "feat", "rows", None)
    col, row = P(None, "rows"), P("rows", None)
    return jax.shard_map(
        body,
        mesh=mesh,
        in_specs=(tok, tok, P(None, "rows", "feat", None), grp, grp, grp, col, row, row, col, col, col, row, row, row, row, col, col),
        out_specs=(grp, tok) + (col,) * 3 + (row,) * 6 + (col,) * 3,
        check_vma=False,
    )
```
